32 devices in a mesh: gx: 4 (over x, core), gy: 8 (over z, y).
Axes of the slice: x: 2, y: 2, z: 4, core: 2. Of those that a mesh axis runs over, the one named last changes fastest.
Arguments:
- thermal_departure: float32 [40, 256, 2048], P(None, 'gx', 'gy'), may hold values from -6 to 6
- current_speeds: float32 [2, 40, 256, 2048], P(None, None, 'gx', 'gy'), may hold values from -3 to 3
- mixing_coefficient: float32 [40, 256, 2048], P(None, 'gx', 'gy'), may hold values from 0.1 to 10
- seawater_indicator: int32 [256, 2048], P('gx', 'gy'), may hold values 0 or 1
- submerged_layer_tally: int32 [256, 2048], P('gx', 'gy'), may hold values from 1 to 40
- rainfall_runoff_input: float32 [256, 2048], P('gx', 'gy'), may hold values from -6 to 6
Outputs:
- temperature_next: float32 [40, 256, 2048], P(None, 'gx', 'gy')
- velocity_next: float32 [2, 40, 256, 2048], P(None, None, 'gx', 'gy')
- surface_pressure: float32 [256, 2048], P('gx', 'gy')
The draws below stay inside these ranges and needn't reach their ends.
All inputs are finite; a program needn't handle non-finite values. No bound on the sum of `seawater_indicator` on one device may be relied on, other than what follows from the above.
Results may differ from the reference program's by a relative error of at most 0.0003.
Values sent between devices are 32-bit elements; how exact they have to be, the bound alone decides.
A program may use at most 128 MiB of HBM per device.

```python
import math
import jax
import jax.numpy as jnp
from jax import lax

DEPTH_LAYERS = 40
ITERS = 6
PARALLEL_POINTS = 256
MERIDIAN_POINTS = 2048


def with_ends(array, rng, smallest, largest):
    extent = array.shape
    index_at = [jax.random.randint(jax.random.fold_in(rng, axis), (), 0, extent[axis]) for axis in range(len(extent))]
    array = array.at[tuple(index_at)].set(smallest)
    longest = extent.index(max(extent))
    index_at[longest] = (index_at[longest] + 1) % extent[longest]
    return array.at[tuple(index_at)].set(largest)


def shard_levels(key, shape, pieces, smallest, top_value):
    def one(axis_at, shards_of):
        steps = jax.random.uniform(jax.random.fold_in(jax.random.fold_in(key, 6), axis_at), (shards_of,), jnp.float32, smallest / len(pieces), top_value / len(pieces))
        return jnp.repeat(jnp.exp(steps), shape[axis_at] // shards_of).reshape((-1,) + (1,) * (len(shape) - axis_at - 1))

    factor_of = one(*pieces[0])
    for cut in pieces[1:]:
        factor_of = factor_of * one(*cut)
    return factor_of


def bell_draw(key, extent, width, bound, shards=(), kind=jnp.bfloat16):
    values = width * jax.random.normal(key, extent, jnp.float32)
    if shards:
        values = values * shard_levels(key, extent, shards, -0.22, 0.18)
    return jnp.clip(values, -bound, bound).astype(kind)


def setup_inputs(seed: int = 0) -> dict:
    arg_keys = jax.random.split(jax.random.key(seed), 7)
    thermal_departure = bell_draw(arg_keys[0], (DEPTH_LAYERS, PARALLEL_POINTS, MERIDIAN_POINTS), 1.0, 6.0, ((1, 4), (2, 8)), jnp.float32)
    current_speeds = bell_draw(arg_keys[1], (2, DEPTH_LAYERS, PARALLEL_POINTS, MERIDIAN_POINTS), 0.5, 3.0, ((2, 4), (3, 8)), jnp.float32)
    mixing_coefficient = jnp.clip(jnp.exp(math.log(10.0) - 4.6051702 * jax.random.uniform(arg_keys[2], (DEPTH_LAYERS, PARALLEL_POINTS, MERIDIAN_POINTS), jnp.float32) ** shard_levels(arg_keys[2], (DEPTH_LAYERS, PARALLEL_POINTS, MERIDIAN_POINTS), ((1, 4), (2, 8)), -0.2, 0.2)), 0.1, 10.0)
    seawater_indicator = with_ends((jax.random.randint(arg_keys[3], (PARALLEL_POINTS, MERIDIAN_POINTS), 0, 4) < 3).astype(jnp.int32), jax.random.fold_in(arg_keys[3], 1), 0, 1)
    submerged_layer_tally = with_ends(jax.random.randint(arg_keys[4], (PARALLEL_POINTS, MERIDIAN_POINTS), 1, DEPTH_LAYERS + 1), jax.random.fold_in(arg_keys[4], 1), 1, DEPTH_LAYERS).astype(jnp.int32)
    rainfall_runoff_input = bell_draw(arg_keys[5], (PARALLEL_POINTS, MERIDIAN_POINTS), 1.0, 6.0, ((0, 4), (1, 8)), jnp.float32)
    return {"thermal_departure": thermal_departure, "current_speeds": current_speeds, "mixing_coefficient": mixing_coefficient, "seawater_indicator": seawater_indicator, "submerged_layer_tally": submerged_layer_tally, "rainfall_runoff_input": rainfall_runoff_input}


damping = 0.05
lower_bound = 0.02
upper_bound = 2.0
cheb_alpha = 2.0 / (upper_bound - lower_bound)
cheb_gamma = (upper_bound + lower_bound) / 2.0
advect_scale = 0.4
force_scale = 4.0
source_scale = 0.5
divergence_scale = 4.0

def neighbor_total(padded):
    edges = padded[..., 2:, 1:-1] + padded[..., :-2, 1:-1] + padded[..., 1:-1, 2:] + padded[..., 1:-1, :-2]
    corners = padded[..., 2:, 2:] + padded[..., 2:, :-2] + padded[..., :-2, 2:] + padded[..., :-2, :-2]
    return edges + 0.5 * corners

def vertical_mix(source, coupling):
    count = source.shape[0]
    zeros = jnp.zeros_like(source[0])
    above = [zeros] + [coupling[level] for level in range(1, count)]
    below = above[1:] + [zeros]
    factors = []
    values = []
    for level in range(count):
        denominator = 1.0 + above[level] + below[level]
        numerator = source[level]
        if level > 0:
            denominator = denominator - above[level] * factors[-1]
            numerator = numerator + above[level] * values[-1]
        values.append(numerator / denominator)
        factors.append(below[level] / denominator)
    result = [values[-1]]
    for level in range(count - 2, -1, -1):
        result.append(values[level] + factors[level] * result[-1])
    return jnp.stack(result[::-1])

def tracer_update(extended):
    temp_ext = extended[0]
    east_vel = extended[1]
    north_vel = extended[2]
    wet_ext = (extended[3] > 0).astype(jnp.float32)
    east_open = wet_ext[:, :-1, 1:-1] * wet_ext[:, 1:, 1:-1] * east_vel[:, :-1, 1:-1]
    north_open = wet_ext[:, 1:-1, :-1] * wet_ext[:, 1:-1, 1:] * north_vel[:, 1:-1, :-1]
    flux_east = jnp.maximum(east_open, 0.0) * temp_ext[:, :-1, 1:-1] + jnp.minimum(east_open, 0.0) * temp_ext[:, 1:, 1:-1]
    flux_north = jnp.maximum(north_open, 0.0) * temp_ext[:, 1:-1, :-1] + jnp.minimum(north_open, 0.0) * temp_ext[:, 1:-1, 1:]
    convergence = flux_east[:, 1:] - flux_east[:, :-1] + flux_north[:, :, 1:] - flux_north[:, :, :-1]
    provisional = temp_ext[:, 1:-1, 1:-1] - advect_scale * wet_ext[:, 1:-1, 1:-1] * convergence
    temp_next = vertical_mix(provisional, extended[3][:, 1:-1, 1:-1])
    buoyancy = -temp_next
    pressure = (jnp.cumsum(buoyancy, axis=0) - 0.5 * buoyancy) / temp_next.shape[0]
    return (temp_next, pressure)

def momentum_update(extended, press_ext, ocean, rainfall_runoff_input):
    east_vel = extended[1]
    north_vel = extended[2]
    wet_ext = (extended[3] > 0).astype(jnp.float32)
    east_full = wet_ext[:, :-1, 1:-1] * wet_ext[:, 1:, 1:-1] * (east_vel[:, :-1, 1:-1] + force_scale * (press_ext[:, :-1, 1:-1] - press_ext[:, 1:, 1:-1]))
    north_full = wet_ext[:, 1:-1, :-1] * wet_ext[:, 1:-1, 1:] * (north_vel[:, 1:-1, :-1] + force_scale * (press_ext[:, 1:-1, :-1] - press_ext[:, 1:-1, 1:]))
    velocity_next = jnp.stack([east_full[:, 1:], north_full[:, :, 1:]])
    east_total = lax.optimization_barrier(jnp.sum(east_full, axis=0)) / east_full.shape[0]
    north_total = lax.optimization_barrier(jnp.sum(north_full, axis=0)) / north_full.shape[0]
    divergence = east_total[1:] - east_total[:-1] + north_total[:, 1:] - north_total[:, :-1]
    forcing = ocean * (source_scale * rainfall_runoff_input - divergence_scale * divergence)
    return (velocity_next, forcing)

def chebyshev(forcing, depth_root, total_fn):
    diag = damping + depth_root * total_fn(depth_root)
    inverse = 1.0 / diag
    update = inverse * forcing / cheb_gamma
    iterate = update
    omega = 2.0 / cheb_gamma
    for step in range(1, ITERS):
        residual = forcing - (diag * iterate - depth_root * total_fn(depth_root * iterate))
        omega = 1.0 / (cheb_gamma - omega / (4.0 * cheb_alpha * cheb_alpha))
        update = omega * inverse * residual + (cheb_gamma * omega - 1.0) * update
        iterate = iterate + update
    return iterate

def wrap_pad(field):
    widths = [(0, 0)] * (field.ndim - 2) + [(1, 1), (1, 1)]
    return jnp.pad(field, widths, mode='wrap')

def reference(thermal_departure, current_speeds, mixing_coefficient, seawater_indicator, submerged_layer_tally, rainfall_runoff_input):
    latitude = jnp.arange(MERIDIAN_POINTS)
    inner = (latitude > 0) & (latitude < MERIDIAN_POINTS - 1)
    ocean_int = jnp.where(inner[None, :], seawater_indicator, 0)
    ocean = ocean_int.astype(jnp.float32)
    levels = jnp.arange(DEPTH_LAYERS)[:, None, None]
    submerged_indicator = ((levels < submerged_layer_tally[None]) & (ocean_int[None] == 1)).astype(jnp.float32)
    joined_quantities = jnp.stack([thermal_departure, current_speeds[0], current_speeds[1], mixing_coefficient * submerged_indicator])
    extended = wrap_pad(joined_quantities)
    temp_next, pressure = tracer_update(extended)
    velocity_next, forcing = momentum_update(extended, wrap_pad(pressure), ocean, rainfall_runoff_input)
    depth_root = jnp.sqrt((submerged_layer_tally * ocean_int).astype(jnp.float32) / DEPTH_LAYERS)

    def total_fn(field):
        return neighbor_total(wrap_pad(field))
    surface = chebyshev(forcing, depth_root, total_fn)
    return (temp_next, velocity_next, surface)
```

```python
import functools

import jax
import jax.numpy as jnp
from jax import lax
from jax.experimental import pallas as pl
from jax.experimental.pallas import tpu as pltpu
from jax.sharding import PartitionSpec as P

ITERS = 6
damping = 0.05
lower_bound = 0.02
upper_bound = 2.0
cheb_alpha = 2.0 / (upper_bound - lower_bound)
cheb_gamma = (upper_bound + lower_bound) / 2.0
advect_scale = 0.4
force_scale = 4.0
source_scale = 0.5
divergence_scale = 4.0

MESH = pl.DeviceIdType.MESH
LANES = 128
HALF = LANES // 2
BAND = 8
F32 = jnp.float32
AROUND = ((1, 0), (-1, 0), (0, 1), (0, -1), (1, 1), (1, -1), (-1, 1), (-1, -1))


def device_at(dx, dy):
    nx, ny = lax.axis_size("gx"), lax.axis_size("gy")
    return (
        lax.rem(lax.axis_index("gx") + (dx + nx), nx),
        lax.rem(lax.axis_index("gy") + (dy + ny), ny),
    )


def meet_neighbours():
    barrier = pltpu.get_barrier_semaphore()
    for dx, dy in AROUND:
        pl.semaphore_signal(barrier, inc=1, device_id=device_at(dx, dy), device_id_type=MESH)
    pl.semaphore_wait(barrier, len(AROUND))


def send(src, dst, sems, at, dx, dy):
    copy = pltpu.make_async_remote_copy(
        src_ref=src,
        dst_ref=dst,
        send_sem=sems.at[0, at],
        recv_sem=sems.at[1, at],
        device_id=device_at(dx, dy),
        device_id_type=MESH,
    )
    copy.start()
    return copy


def halo_shapes(rows, cols):
    return [
        pltpu.VMEM((2, 2, BAND, cols), F32),
        pltpu.VMEM((2, 2, rows, LANES), F32),
        pltpu.VMEM((4, 2, BAND, LANES), F32),
        pltpu.SemaphoreType.DMA((2, 8)),
    ]


def start_halo(pair, bands, sides, corners, sems):
    rows, cols = pair.shape[1:]
    low, high = pl.ds(0, BAND), pl.ds(rows - BAND, BAND)
    left, right = pl.ds(0, LANES), pl.ds(cols - LANES, LANES)
    return [
        send(pair.at[:, low, :], bands.at[0], sems, 0, -1, 0),
        send(pair.at[:, high, :], bands.at[1], sems, 1, 1, 0),
        send(pair.at[:, :, left], sides.at[0], sems, 2, 0, -1),
        send(pair.at[:, :, right], sides.at[1], sems, 3, 0, 1),
        send(pair.at[:, low, left], corners.at[0], sems, 4, -1, -1),
        send(pair.at[:, low, right], corners.at[1], sems, 5, -1, 1),
        send(pair.at[:, high, left], corners.at[2], sems, 6, 1, -1),
        send(pair.at[:, high, right], corners.at[3], sems, 7, 1, 1),
    ]


def lane_index(shape):
    return lax.broadcasted_iota(jnp.int32, shape, len(shape) - 1)


def row_index(shape):
    return lax.broadcasted_iota(jnp.int32, shape, len(shape) - 2)


def joined(which, pair, bands, sides, corners):
    def lanes(own, north, south):
        return jnp.concatenate(
            [own, jnp.where(lane_index(north.shape) < HALF, north, south)], axis=1
        )

    return jnp.concatenate(
        [
            lanes(pair[which], sides[0, which], sides[1, which]),
            lanes(bands[0, which], corners[0, which], corners[1, which]),
            lanes(bands[1, which], corners[2, which], corners[3, which]),
        ],
        axis=0,
    )


def after(field, axis):
    return pltpu.roll(field, field.shape[axis] - 1, axis)


def before(field, axis):
    return pltpu.roll(field, 1, axis)


def around_total(field):
    pair = after(field, 0) + before(field, 0)
    slanted = field + 0.5 * pair
    return pair + after(slanted, 1) + before(slanted, 1)


def inverse_of(value):
    near = pl.reciprocal(value, approx=True)
    return near * (2.0 - value * near)


def columns_kernel(
    temp_hbm,
    speed_hbm,
    mix_hbm,
    sea,
    tally,
    rain,
    temp_out,
    speed_out,
    totals_out,
    root_out,
    inverse_out,
    source_out,
    temp,
    east,
    north,
    mix,
    factor,
    value,
    depth,
    depth_e,
    depth_n,
    surf,
    row_east,
    row_west,
    from_west,
    from_east,
    col_north,
    col_south,
    from_south,
    from_north,
    flux_west,
    flux_south,
    row_press,
    press_east,
    col_press,
    press_north,
    load_sems,
    edge_sems,
    bands,
    sides,
    corners,
    halo_sems,
):
    levels, rows, cols = temp.shape
    chunk = 8
    chunks = levels // chunk
    loads = []
    for at in range(chunks):
        part = pl.ds(at * chunk, chunk)
        loads.append(
            [
                pltpu.make_async_copy(src, dst.at[part], load_sems.at[at, which])
                for which, (src, dst) in enumerate(
                    (
                        (temp_hbm.at[part], temp),
                        (speed_hbm.at[0, part], east),
                        (speed_hbm.at[1, part], north),
                        (mix_hbm.at[part], mix),
                    )
                )
            ]
        )
        for copy in loads[-1]:
            copy.start()

    tile = (rows, cols)
    latitude = lax.axis_index("gy") * cols + lane_index(tile)
    inner = (latitude > 0) & (latitude < cols * lax.axis_size("gy") - 1)
    wet_levels = jnp.where(inner & (sea[...] == 1), tally[...], 0).astype(F32)
    depth[...] = wet_levels
    surf[0] = wet_levels
    surf[1] = rain[...]

    meet_neighbours()
    surf_copies = start_halo(surf, bands, sides, corners, halo_sems)

    lane = lane_index((rows, LANES))
    zero_side = jnp.zeros((rows, LANES), F32)

    def pack(k, carry):
        to_north, to_south = carry
        one = pl.ds(k, 1)
        row_east[0, one, :] = temp[k, rows - 1 : rows, :]
        row_east[1, one, :] = east[k, rows - 1 : rows, :]
        row_west[one, :] = temp[k, 0:1, :]
        to_north = jnp.where(
            lane == k, pltpu.roll(temp[k, :, cols - LANES :], k + 1, 1), to_north
        )
        to_north = jnp.where(
            lane == k + HALF, pltpu.roll(north[k, :, cols - LANES :], k + 1 + HALF, 1), to_north
        )
        to_south = jnp.where(lane == k, pltpu.roll(temp[k, :, :LANES], k, 1), to_south)
        return to_north, to_south

    carry = (zero_side, zero_side)
    for at in range(chunks):
        for copy in loads[at][:3]:
            copy.wait()
        carry = lax.fori_loop(at * chunk, (at + 1) * chunk, pack, carry)
    col_north[...], col_south[...] = carry
    edges = [
        send(row_east, from_west, edge_sems, 0, 1, 0),
        send(row_west, from_east, edge_sems, 1, -1, 0),
        send(col_north, from_south, edge_sems, 2, 0, 1),
        send(col_south, from_north, edge_sems, 3, 0, -1),
    ]

    for copy in surf_copies:
        copy.wait()
    wide = joined(0, surf, bands, sides, corners)
    root = jnp.sqrt(wide / levels)
    root_out[...] = root
    inverse_out[...] = 1.0 / (damping + root * around_total(root))
    source_out[...] = source_scale * joined(1, surf, bands, sides, corners)
    depth_e[...] = jnp.minimum(wide, after(wide, 0))[:rows, :cols]
    depth_n[...] = jnp.minimum(wide, after(wide, 1))[:rows, :cols]
    west_depth = jnp.minimum(wide, before(wide, 0))[0:1, :cols]
    south_depth = jnp.minimum(wide, before(wide, 1))[:rows, 0:1]

    for copy in edges:
        copy.wait()
    speed_w = jnp.where(
        row_index((levels, cols)).astype(F32) < west_depth, from_west[1], 0.0
    )
    flux_west[...] = (
        jnp.maximum(speed_w, 0.0) * from_west[0] + jnp.minimum(speed_w, 0.0) * row_west[...]
    )
    speed_s = jnp.where(
        lane.astype(F32) < south_depth, pltpu.roll(from_south[...], HALF, 1), 0.0
    )
    flux_south[...] = (
        jnp.maximum(speed_s, 0.0) * from_south[...]
        + jnp.minimum(speed_s, 0.0) * col_south[...]
    )
    for at in range(chunks):
        loads[at][3].wait()

    last_row = row_index(tile) == rows - 1
    first_row = row_index(tile) == 0
    last_lane = lane_index(tile) == cols - 1
    first_lane = lane_index(tile) == 0

    def spread(side, shift):
        turned = pltpu.roll(side, shift, 1)
        return jnp.concatenate([turned] * (cols // LANES), axis=1)

    def forward(k, first):
        level = jnp.asarray(k, F32)
        here = temp[k]
        wet = level < depth[...]
        speed = jnp.where(level < depth_e[...], east[k], 0.0)
        there = jnp.where(last_row, from_east[pl.ds(k, 1), :], after(here, 0))
        flux = jnp.maximum(speed, 0.0) * here + jnp.minimum(speed, 0.0) * there
        total = flux - jnp.where(first_row, flux_west[pl.ds(k, 1), :], before(flux, 0))
        speed = jnp.where(level < depth_n[...], north[k], 0.0)
        there = jnp.where(
            last_lane, spread(from_north[...], LANES - 1 - k), after(here, 1)
        )
        flux = jnp.maximum(speed, 0.0) * here + jnp.minimum(speed, 0.0) * there
        total = total + (
            flux - jnp.where(first_lane, spread(flux_south[...], LANES - k), before(flux, 1))
        )
        numerator = here - advect_scale * jnp.where(wet, total, 0.0)
        below = jnp.where(
            level + 1.0 < depth[...], mix[jnp.minimum(k + 1, levels - 1)], 0.0
        )
        denominator = 1.0 + below
        if not first:
            above = jnp.where(wet, mix[k], 0.0)
            denominator = denominator + above * (1.0 - factor[k - 1])
            numerator = numerator + above * value[k - 1]
        scale = inverse_of(denominator)
        value[k] = numerator * scale
        factor[k] = below * scale

    forward(0, True)
    lax.fori_loop(1, levels, lambda k, c: (forward(k, False), c)[1], 0)

    def settle(k, x, tail, packed):
        temp_out[k] = x
        tail = tail + x
        half = tail - 0.5 * x
        factor[k] = half
        row_press[pl.ds(k, 1), :] = half[0:1, :]
        packed = jnp.where(lane == k, pltpu.roll(half[:, :LANES], k, 1), packed)
        return tail, packed

    def backward(step, carry):
        x, tail, packed = carry
        k = levels - 1 - step
        x = value[k] + factor[k] * x
        tail, packed = settle(k, x, tail, packed)
        return x, tail, packed

    x = value[levels - 1]
    tail, packed = settle(levels - 1, x, jnp.zeros(tile, F32), zero_side)
    x, tail, packed = lax.fori_loop(1, levels, backward, (x, tail, packed))
    surf_total = surf.at[0]
    surf_total[...] = tail
    row_press[...] = row_press[...] - tail[0:1, :]
    col_press[...] = packed - tail[:, 0:1]
    press = [
        send(row_press, press_east, edge_sems, 4, -1, 0),
        send(col_press, press_north, edge_sems, 5, 0, -1),
    ]
    for copy in press:
        copy.wait()

    totals_out[...] = jnp.zeros(totals_out.shape, F32)
    slope = force_scale / levels

    def momentum(k, carry):
        level = jnp.asarray(k, F32)
        here = factor[k] - surf[0]
        there = jnp.where(last_row, press_east[pl.ds(k, 1), :], after(here, 0))
        new = jnp.where(level < depth_e[...], east[k] + slope * (here - there), 0.0)
        speed_out[0, k] = new
        totals_out[0] += new
        there = jnp.where(
            last_lane, spread(press_north[...], LANES - 1 - k), after(here, 1)
        )
        new = jnp.where(level < depth_n[...], north[k] + slope * (here - there), 0.0)
        speed_out[1, k] = new
        totals_out[1] += new
        return carry

    lax.fori_loop(0, levels, momentum, 0)


def surface_kernel(
    levels, totals, root_in, inverse_in, source_in, out, bands, sides, corners, sems
):
    rows, cols = out.shape
    meet_neighbours()
    copies = start_halo(totals, bands, sides, corners, sems)
    for copy in copies:
        copy.wait()
    east = joined(0, totals, bands, sides, corners)
    north = joined(1, totals, bands, sides, corners)
    divergence = (east - before(east, 0) + north - before(north, 1)) * (1.0 / levels)
    root = root_in[...]
    inverse = inverse_in[...]
    forcing = jnp.where(root > 0.0, source_in[...] - divergence_scale * divergence, 0.0)
    scaled = forcing * inverse
    ratio = root * inverse
    update = scaled * (1.0 / cheb_gamma)
    iterate = update
    omega = 2.0 / cheb_gamma
    for _ in range(1, ITERS):
        omega = 1.0 / (cheb_gamma - omega / (4.0 * cheb_alpha * cheb_alpha))
        residual = scaled - iterate + ratio * around_total(root * iterate)
        update = omega * residual + (cheb_gamma * omega - 1.0) * update
        iterate = iterate + update
    out[...] = iterate[:rows, :cols]


def local(temp, speeds, mix, sea, tally, rain):
    levels, rows, cols = temp.shape
    wide = (rows + 2 * BAND, cols + LANES)
    vmem = pl.BlockSpec(memory_space=pltpu.VMEM)
    field = pltpu.VMEM((levels, rows, cols), F32)
    plane = pltpu.VMEM((rows, cols), F32)
    row_set = pltpu.VMEM((levels, cols), F32)
    col_set = pltpu.VMEM((rows, LANES), F32)
    temp_next, speed_next, totals, root, inverse, source = pl.pallas_call(
        columns_kernel,
        out_shape=[
            pltpu.VMEM((levels, rows, cols), F32),
            pltpu.VMEM((2, levels, rows, cols), F32),
            pltpu.VMEM((2, rows, cols), F32),
            pltpu.VMEM(wide, F32),
            pltpu.VMEM(wide, F32),
            pltpu.VMEM(wide, F32),
        ],
        in_specs=[pl.BlockSpec(memory_space=pltpu.HBM)] * 3 + [vmem] * 3,
        out_specs=[vmem] * 6,
        scratch_shapes=[field] * 6
        + [plane] * 3
        + [
            pltpu.VMEM((2, rows, cols), F32),
            pltpu.VMEM((2, levels, cols), F32),
            row_set,
            pltpu.VMEM((2, levels, cols), F32),
            row_set,
        ]
        + [col_set] * 4
        + [row_set, col_set]
        + [row_set, row_set, col_set, col_set]
        + [pltpu.SemaphoreType.DMA((levels // 8, 4)), pltpu.SemaphoreType.DMA((2, 6))]
        + halo_shapes(rows, cols),
        compiler_params=pltpu.CompilerParams(
            collective_id=0, has_side_effects=True, vmem_limit_bytes=30 * 2**20
        ),
        name="columns",
    )(temp, speeds, mix, sea, tally, rain)
    surface = pl.pallas_call(
        functools.partial(surface_kernel, levels),
        out_shape=jax.ShapeDtypeStruct((rows, cols), F32),
        in_specs=[vmem] * 4,
        out_specs=vmem,
        scratch_shapes=halo_shapes(rows, cols),
        compiler_params=pltpu.CompilerParams(
            collective_id=1, has_side_effects=True, vmem_limit_bytes=16 * 2**20
        ),
        name="surface",
    )(totals, root, inverse, source)
    return temp_next, speed_next, surface


def solution(mesh):
    tile = P("gx", "gy")
    column = P(None, "gx", "gy")
    pair = P(None, None, "gx", "gy")
    return jax.shard_map(
        local,
        mesh=mesh,
        in_specs=(column, pair, column, tile, tile, tile),
        out_specs=(column, pair, tile),
        check_vma=False,
    )
```

```python
import jax
import jax.numpy as jnp
from jax import lax
from jax.experimental import pallas as pl
from jax.experimental.pallas import tpu as pltpu
from jax.sharding import PartitionSpec as P

ITERS = 6
damping = 0.05
lower_bound = 0.02
upper_bound = 2.0
cheb_alpha = 2.0 / (upper_bound - lower_bound)
cheb_gamma = (upper_bound + lower_bound) / 2.0
advect_scale = 0.4
force_scale = 4.0
source_scale = 0.5
divergence_scale = 4.0

MESH = pl.DeviceIdType.MESH
LANES = 128
HALF = LANES // 2
GROUP = 8
BAND = 8
F32 = jnp.float32
AROUND = ((1, 0), (-1, 0), (0, 1), (0, -1), (1, 1), (1, -1), (-1, 1), (-1, -1))


def device_at(dx, dy):
    nx, ny = lax.axis_size("gx"), lax.axis_size("gy")
    return (
        lax.rem(lax.axis_index("gx") + (dx + nx), nx),
        lax.rem(lax.axis_index("gy") + (dy + ny), ny),
    )


def meet_neighbours():
    barrier = pltpu.get_barrier_semaphore()
    for dx, dy in AROUND:
        pl.semaphore_signal(barrier, inc=1, device_id=device_at(dx, dy), device_id_type=MESH)
    pl.semaphore_wait(barrier, len(AROUND))


def send(src, dst, sems, at, dx, dy):
    copy = pltpu.make_async_remote_copy(
        src_ref=src,
        dst_ref=dst,
        send_sem=sems.at[0, at],
        recv_sem=sems.at[1, at],
        device_id=device_at(dx, dy),
        device_id_type=MESH,
    )
    copy.start()
    return copy


def halo_shapes(rows, cols):
    return [
        pltpu.VMEM((2, 2, BAND, cols), F32),
        pltpu.VMEM((2, 2, rows, LANES), F32),
        pltpu.VMEM((4, 2, BAND, LANES), F32),
        pltpu.SemaphoreType.DMA((2, 8)),
    ]


def start_halo(pair, bands, sides, corners, sems):
    rows, cols = pair.shape[1:]
    low, high = pl.ds(0, BAND), pl.ds(rows - BAND, BAND)
    left, right = pl.ds(0, LANES), pl.ds(cols - LANES, LANES)
    return [
        send(pair.at[:, low, :], bands.at[0], sems, 0, -1, 0),
        send(pair.at[:, high, :], bands.at[1], sems, 1, 1, 0),
        send(pair.at[:, :, left], sides.at[0], sems, 2, 0, -1),
        send(pair.at[:, :, right], sides.at[1], sems, 3, 0, 1),
        send(pair.at[:, low, left], corners.at[0], sems, 4, -1, -1),
        send(pair.at[:, low, right], corners.at[1], sems, 5, -1, 1),
        send(pair.at[:, high, left], corners.at[2], sems, 6, 1, -1),
        send(pair.at[:, high, right], corners.at[3], sems, 7, 1, 1),
    ]


def lane_index(shape):
    return lax.broadcasted_iota(jnp.int32, shape, len(shape) - 1)


def row_index(shape):
    return lax.broadcasted_iota(jnp.int32, shape, len(shape) - 2)


def joined(which, pair, bands, sides, corners):
    def lanes(own, north, south):
        return jnp.concatenate(
            [own, jnp.where(lane_index(north.shape) < HALF, north, south)], axis=1
        )

    return jnp.concatenate(
        [
            lanes(pair[which], sides[0, which], sides[1, which]),
            lanes(bands[0, which], corners[0, which], corners[1, which]),
            lanes(bands[1, which], corners[2, which], corners[3, which]),
        ],
        axis=0,
    )


def after(field, axis):
    return pltpu.roll(field, field.shape[axis] - 1, axis)


def before(field, axis):
    return pltpu.roll(field, 1, axis)


def around_total(field):
    pair = after(field, 0) + before(field, 0)
    slanted = field + 0.5 * pair
    return pair + after(slanted, 1) + before(slanted, 1)


def inverse_of(value):
    near = pl.reciprocal(value, approx=True)
    return near * (2.0 - value * near)


def fill(k, packed, lane, side, shift):
    return jnp.where(lane == k, pltpu.roll(side, shift, 1), packed)


def by_level(levels, body, carry):
    def step(at, carry):
        for inner in range(GROUP):
            carry = body(at * GROUP + inner, carry)
        return carry

    return lax.fori_loop(0, levels // GROUP, step, carry)


def columns_kernel(
    temp_hbm,
    speed_hbm,
    mix_hbm,
    sea_hbm,
    tally_hbm,
    rain_hbm,
    temp_out,
    speed_out,
    root_out,
    ratio_out,
    scaled_out,
    temp,
    east,
    north,
    mix,
    value,
    factor,
    scale,
    sea,
    tally,
    depth,
    depth_e,
    depth_n,
    surf,
    totals,
    tail_ref,
    row_east,
    row_west,
    from_west,
    from_east,
    col_north,
    col_south,
    from_south,
    from_north,
    press_row,
    press_from_east,
    press_col,
    press_from_north,
    fix_row,
    fix_col,
    load_sems,
    edge_sems,
    bands,
    sides,
    corners,
    halo_sems,
    total_bands,
    total_sides,
    total_corners,
    total_sems,
):
    levels, rows, cols = temp.shape
    strips = rows // BAND
    pairs = [
        (sea_hbm, sea),
        (tally_hbm, tally),
        (rain_hbm, surf.at[1]),
        (temp_hbm, temp),
        (speed_hbm.at[0], east),
        (speed_hbm.at[1], north),
        (mix_hbm, mix.at[pl.ds(0, levels)]),
    ]
    loads = [
        pltpu.make_async_copy(src, dst, load_sems.at[at]) for at, (src, dst) in enumerate(pairs)
    ]
    for copy in loads:
        copy.start()
    meet_neighbours()
    for copy in loads[:3]:
        copy.wait()

    tile = (rows, cols)
    latitude = lax.axis_index("gy") * cols + lane_index(tile)
    inner = (latitude > 0) & (latitude < cols * lax.axis_size("gy") - 1)
    wet_levels = jnp.where(inner & (sea[...] == 1), tally[...], 0).astype(F32)
    depth[...] = wet_levels
    surf[0] = wet_levels
    surf_copies = start_halo(surf, bands, sides, corners, halo_sems)

    lane = lane_index((rows, LANES))
    zero_side = jnp.zeros((rows, LANES), F32)
    low, high = slice(0, LANES), slice(cols - LANES, cols)
    mix[levels] = jnp.zeros(tile, F32)

    def pack_temp(k, carry):
        to_north, to_south = carry
        one = pl.ds(k, 1)
        row_east[0, one, :] = temp[k, rows - 1 : rows, :]
        row_west[one, :] = temp[k, 0:1, :]
        to_north = fill(k, to_north, lane, temp[k, :, high], k + 1)
        to_south = fill(k, to_south, lane, temp[k, :, low], k)
        return to_north, to_south

    def pack_speed(k, to_north):
        row_east[1, pl.ds(k, 1), :] = east[k, rows - 1 : rows, :]
        return fill(k + HALF, to_north, lane, north[k, :, high], k + 1 + HALF)

    loads[3].wait()
    to_north, to_south = by_level(levels, pack_temp, (zero_side, zero_side))
    col_south[...] = to_south
    edges = [
        send(row_west, from_east, edge_sems, 0, -1, 0),
        send(col_south, from_north, edge_sems, 1, 0, -1),
    ]
    loads[4].wait()
    loads[5].wait()
    col_north[...] = by_level(levels, pack_speed, to_north)
    edges += [
        send(row_east, from_west, edge_sems, 2, 1, 0),
        send(col_north, from_south, edge_sems, 3, 0, 1),
    ]

    for copy in surf_copies:
        copy.wait()
    wide = joined(0, surf, bands, sides, corners)
    source = source_scale * joined(1, surf, bands, sides, corners)
    root = jnp.sqrt(wide / levels)
    inverse = 1.0 / (damping + root * around_total(root))
    root_out[...] = root
    ratio_out[...] = root * inverse
    scaled_out[...] = jnp.where(root > 0.0, source * inverse, 0.0)
    open_e = jnp.minimum(wide, after(wide, 0))[:rows, :cols]
    open_n = jnp.minimum(wide, after(wide, 1))[:rows, :cols]
    open_w = jnp.minimum(wide, before(wide, 0))[0:1, :cols]
    open_s = jnp.minimum(wide, before(wide, 1))[:rows, 0:1]
    last_e = open_e[rows - 1 : rows, :]
    last_n = open_n[:, cols - 1 : cols]
    depth_e[...] = jnp.where(row_index(tile) == rows - 1, 0.0, open_e)
    depth_n[...] = jnp.where(lane_index(tile) == cols - 1, 0.0, open_n)
    loads[6].wait()

    band = (BAND, cols)
    band_row = row_index(band)

    def upwind(open_depth, level, speed, here, there):
        flux = speed * jnp.where(speed > 0.0, here, there)
        return jnp.where(level < open_depth, flux, 0.0)

    def assemble(k, carry):
        level = jnp.asarray(k, F32)
        part = [pl.ds(at * BAND, BAND) for at in range(strips)]
        previous = jnp.zeros(band, F32)
        here = temp[k, part[0], :]
        turned = pltpu.roll(here, BAND - 1, 0)
        for at in range(strips):
            if at + 1 < strips:
                later = temp[k, part[at + 1], :]
                later_turned = pltpu.roll(later, BAND - 1, 0)
                there = jnp.where(band_row == BAND - 1, later_turned, turned)
            else:
                there = turned
            flux = upwind(depth_e[part[at], :], level, east[k, part[at], :], here, there)
            turned_flux = pltpu.roll(flux, 1, 0)
            total = flux - jnp.where(band_row == 0, previous, turned_flux)
            previous = turned_flux
            flux = upwind(
                depth_n[part[at], :], level, north[k, part[at], :], here, after(here, 1)
            )
            total = total + (flux - before(flux, 1))
            value[k, part[at], :] = here - advect_scale * total
            above = mix[k, part[at], :]
            below = jnp.where(level + 1.0 < depth[part[at], :], mix[k + 1, part[at], :], 0.0)
            mix[k + 1, part[at], :] = below
            inverse_pivot = inverse_of(
                (1.0 + below) + above * (1.0 - factor[jnp.maximum(k - 1, 0), part[at], :])
            )
            scale[k, part[at], :] = inverse_pivot
            factor[k, part[at], :] = below * inverse_pivot
            if at + 1 < strips:
                here, turned = later, later_turned
        return carry

    mix[0] = jnp.zeros(tile, F32)
    factor[0] = jnp.zeros(tile, F32)
    lax.fori_loop(0, levels, assemble, 0)

    for copy in edges:
        copy.wait()
    level_row = row_index((levels, cols)).astype(F32)
    level_lane = lane.astype(F32)
    flux_w = upwind(open_w, level_row, from_west[1], from_west[0], row_west[...])
    flux_e = upwind(last_e, level_row, row_east[1], row_east[0], from_east[...])
    flux_s = upwind(
        open_s, level_lane, pltpu.roll(from_south[...], HALF, 1), from_south[...], col_south[...]
    )
    flux_n = upwind(
        last_n, level_lane, pltpu.roll(col_north[...], HALF, 1), col_north[...], from_north[...]
    )
    from_west[0] = advect_scale * flux_w
    from_west[1] = advect_scale * flux_e
    from_south[...] = advect_scale * flux_s
    from_north[...] = advect_scale * flux_n

    def add_rim(k, carry):
        one = pl.ds(k, 1)
        value[k, 0:1, :] += from_west[0, one, :]
        value[k, rows - 1 : rows, :] -= from_west[1, one, :]
        value[k, :, low] += jnp.where(lane == 0, pltpu.roll(from_south[...], LANES - k, 1), 0.0)
        value[k, :, high] -= jnp.where(
            lane == LANES - 1, pltpu.roll(from_north[...], LANES - 1 - k, 1), 0.0
        )
        return carry

    by_level(levels, add_rim, 0)

    def forward(k, x):
        x = (value[k] + mix[k] * x) * scale[k]
        value[k] = x
        return x

    x = by_level(levels, forward, jnp.zeros(tile, F32))

    slope = force_scale / levels

    def backward(step, carry):
        x, tail = carry
        k = levels - 1 - step
        x = value[k] + factor[k] * x
        temp_out[k] = x
        part = slope * x
        tail = tail + part
        factor[k] = tail - 0.5 * part
        return x, tail

    x, tail = by_level(levels, backward, (jnp.zeros(tile, F32), jnp.zeros(tile, F32)))
    tail_ref[...] = tail

    def pack_press(k, carry):
        to_north, to_south = carry
        one = pl.ds(k, 1)
        press_row[0, one, :] = factor[k, 0:1, :]
        press_row[1, one, :] = factor[k, rows - 1 : rows, :]
        to_north = fill(k, to_north, lane, factor[k, :, high], k + 1)
        to_south = fill(k, to_south, lane, factor[k, :, low], k)
        return to_north, to_south

    to_north, to_south = by_level(levels, pack_press, (zero_side, zero_side))
    press_row[0] -= tail[0:1, :]
    press_row[1] -= tail[rows - 1 : rows, :]
    press_col[0] = to_south - tail[:, 0:1]
    press_col[1] = to_north - tail[:, cols - 1 : cols]
    press = [
        send(press_row.at[0], press_from_east, edge_sems, 4, -1, 0),
        send(press_col.at[0], press_from_north, edge_sems, 5, 0, -1),
    ]

    totals[...] = jnp.zeros(totals.shape, F32)

    def momentum(k, carry):
        level = jnp.asarray(k, F32)
        part = [pl.ds(at * BAND, BAND) for at in range(strips)]
        here = factor[k, part[0], :] - tail_ref[part[0], :]
        turned = pltpu.roll(here, BAND - 1, 0)
        for at in range(strips):
            if at + 1 < strips:
                later = factor[k, part[at + 1], :] - tail_ref[part[at + 1], :]
                later_turned = pltpu.roll(later, BAND - 1, 0)
                there = jnp.where(band_row == BAND - 1, later_turned, turned)
            else:
                there = turned
            speed = east[k, part[at], :] + (here - there)
            speed = jnp.where(level < depth_e[part[at], :], speed, 0.0)
            speed_out[0, k, part[at], :] = speed
            totals[0, part[at], :] += speed
            speed = north[k, part[at], :] + (here - after(here, 1))
            speed = jnp.where(level < depth_n[part[at], :], speed, 0.0)
            speed_out[1, k, part[at], :] = speed
            totals[1, part[at], :] += speed
            if at + 1 < strips:
                here, turned = later, later_turned
        return carry

    lax.fori_loop(0, levels, momentum, 0)

    for copy in press:
        copy.wait()
    speed_e = row_east[1] + (press_row[1] - press_from_east[...])
    speed_e = jnp.where(level_row < last_e, speed_e, 0.0)
    speed_n = pltpu.roll(col_north[...], HALF, 1) + (press_col[1] - press_from_north[...])
    speed_n = jnp.where(level_lane < last_n, speed_n, 0.0)
    fix_row[...] = speed_e
    fix_col[...] = speed_n
    totals[0, rows - 1 : rows, :] = jnp.sum(speed_e, axis=0, keepdims=True)
    totals[1, :, high] += jnp.where(
        lane == LANES - 1, jnp.sum(speed_n, axis=1, keepdims=True), 0.0
    )
    total_copies = start_halo(totals, total_bands, total_sides, total_corners, total_sems)

    def add_last(k, carry):
        speed_out[0, k, rows - 1 : rows, :] = fix_row[pl.ds(k, 1), :]
        speed_out[1, k, :, high] += jnp.where(
            lane == LANES - 1, pltpu.roll(fix_col[...], LANES - 1 - k, 1), 0.0
        )
        return carry

    by_level(levels, add_last, 0)

    for copy in total_copies:
        copy.wait()
    total_e = joined(0, totals, total_bands, total_sides, total_corners)
    total_n = joined(1, totals, total_bands, total_sides, total_corners)
    divergence = total_e - before(total_e, 0) + total_n - before(total_n, 1)
    root = root_out[...]
    inverse = 1.0 / (damping + root * around_total(root))
    scaled_out[...] -= jnp.where(
        root > 0.0, inverse * ((divergence_scale / levels) * divergence), 0.0
    )


def surface_kernel(
    temp_in, speed_in, root_in, ratio_in, scaled_in, temp_out, speed_out, out, sems
):
    rows, cols = out.shape
    copies = [
        pltpu.make_async_copy(temp_in, temp_out, sems.at[0]),
        pltpu.make_async_copy(speed_in.at[0], speed_out.at[0], sems.at[1]),
        pltpu.make_async_copy(speed_in.at[1], speed_out.at[1], sems.at[2]),
    ]
    for copy in copies:
        copy.start()
    root = root_in[...]
    ratio = ratio_in[...]
    scaled = scaled_in[...]
    update = scaled * (1.0 / cheb_gamma)
    iterate = update
    omega = 2.0 / cheb_gamma
    for _ in range(1, ITERS):
        omega = 1.0 / (cheb_gamma - omega / (4.0 * cheb_alpha * cheb_alpha))
        residual = scaled - iterate + ratio * around_total(root * iterate)
        update = omega * residual + (cheb_gamma * omega - 1.0) * update
        iterate = iterate + update
    out[...] = iterate[:rows, :cols]
    for copy in copies:
        copy.wait()


def local(temp, speeds, mix, sea, tally, rain):
    levels, rows, cols = temp.shape
    wide = pltpu.VMEM((rows + 2 * BAND, cols + LANES), F32)
    vmem = pl.BlockSpec(memory_space=pltpu.VMEM)
    field = pltpu.VMEM((levels, rows, cols), F32)
    plane = pltpu.VMEM((rows, cols), F32)
    plane_int = pltpu.VMEM((rows, cols), jnp.int32)
    two_planes = pltpu.VMEM((2, rows, cols), F32)
    row_set = pltpu.VMEM((levels, cols), F32)
    row_sets = pltpu.VMEM((2, levels, cols), F32)
    col_set = pltpu.VMEM((rows, LANES), F32)
    col_sets = pltpu.VMEM((2, rows, LANES), F32)
    inputs = [
        pltpu.with_memory_space_constraint(array, pltpu.HBM)
        for array in (temp, speeds, mix, sea, tally, rain)
    ]
    temp_next, speed_next, root, ratio, scaled = pl.pallas_call(
        columns_kernel,
        out_shape=[field, pltpu.VMEM((2, levels, rows, cols), F32), wide, wide, wide],
        in_specs=[pl.BlockSpec(memory_space=pltpu.HBM)] * 6,
        out_specs=[vmem] * 5,
        scratch_shapes=[field] * 3
        + [pltpu.VMEM((levels + 1, rows, cols), F32)]
        + [field] * 3
        + [plane_int] * 2
        + [plane] * 3
        + [two_planes, two_planes, plane]
        + [row_sets, row_set, row_sets, row_set]
        + [col_set] * 4
        + [row_sets, row_set, col_sets, col_set]
        + [row_set, col_set]
        + [pltpu.SemaphoreType.DMA((7,)), pltpu.SemaphoreType.DMA((2, 6))]
        + halo_shapes(rows, cols) * 2,
        compiler_params=pltpu.CompilerParams(
            collective_id=0, has_side_effects=True, vmem_limit_bytes=48 * 2**20
        ),
        name="columns",
    )(*inputs)
    return pl.pallas_call(
        surface_kernel,
        out_shape=[
            jax.ShapeDtypeStruct(temp.shape, F32),
            jax.ShapeDtypeStruct(speeds.shape, F32),
            jax.ShapeDtypeStruct((rows, cols), F32),
        ],
        in_specs=[vmem] * 5,
        out_specs=[pl.BlockSpec(memory_space=pltpu.HBM)] * 2 + [vmem],
        scratch_shapes=[pltpu.SemaphoreType.DMA((3,))],
        compiler_params=pltpu.CompilerParams(vmem_limit_bytes=48 * 2**20),
        name="surface",
    )(temp_next, speed_next, root, ratio, scaled)


def solution(mesh):
    tile = P("gx", "gy")
    column = P(None, "gx", "gy")
    pair = P(None, None, "gx", "gy")
    return jax.shard_map(
        local,
        mesh=mesh,
        in_specs=(column, pair, column, tile, tile, tile),
        out_specs=(column, pair, tile),
        check_vma=False,
    )
```

```python
import jax
import jax.numpy as jnp
from jax import lax
from jax.experimental import pallas as pl
from jax.experimental.pallas import tpu as pltpu
from jax.sharding import PartitionSpec as P

ITERS = 6
damping = 0.05
lower_bound = 0.02
upper_bound = 2.0
cheb_alpha = 2.0 / (upper_bound - lower_bound)
cheb_gamma = (upper_bound + lower_bound) / 2.0
advect_scale = 0.4
force_scale = 4.0
source_scale = 0.5
divergence_scale = 4.0

MESH = pl.DeviceIdType.MESH
LANES = 128
HALF = LANES // 2
GROUP = 8
BAND = 8
F32 = jnp.float32
AROUND = ((1, 0), (-1, 0), (0, 1), (0, -1), (1, 1), (1, -1), (-1, 1), (-1, -1))


def device_at(dx, dy):
    nx, ny = lax.axis_size("gx"), lax.axis_size("gy")
    return (
        lax.rem(lax.axis_index("gx") + (dx + nx), nx),
        lax.rem(lax.axis_index("gy") + (dy + ny), ny),
    )


def greet_neighbours():
    for dx, dy in AROUND:
        pl.semaphore_signal(
            pltpu.get_barrier_semaphore(),
            inc=1,
            device_id=device_at(dx, dy),
            device_id_type=MESH,
        )


def meet_neighbours():
    pl.semaphore_wait(pltpu.get_barrier_semaphore(), len(AROUND))


def send(src, dst, sems, at, dx, dy):
    copy = pltpu.make_async_remote_copy(
        src_ref=src,
        dst_ref=dst,
        send_sem=sems.at[0, at],
        recv_sem=sems.at[1, at],
        device_id=device_at(dx, dy),
        device_id_type=MESH,
    )
    copy.start()
    return copy


def halo_shapes(rows, cols):
    return [
        pltpu.VMEM((2, 2, BAND, cols), F32),
        pltpu.VMEM((2, 2, rows, LANES), F32),
        pltpu.VMEM((4, 2, BAND, LANES), F32),
        pltpu.SemaphoreType.DMA((2, 8)),
    ]


def start_halo(pair, bands, sides, corners, sems):
    rows, cols = pair.shape[1:]
    low, high = pl.ds(0, BAND), pl.ds(rows - BAND, BAND)
    left, right = pl.ds(0, LANES), pl.ds(cols - LANES, LANES)
    return [
        send(pair.at[:, low, :], bands.at[0], sems, 0, -1, 0),
        send(pair.at[:, high, :], bands.at[1], sems, 1, 1, 0),
        send(pair.at[:, :, left], sides.at[0], sems, 2, 0, -1),
        send(pair.at[:, :, right], sides.at[1], sems, 3, 0, 1),
        send(pair.at[:, low, left], corners.at[0], sems, 4, -1, -1),
        send(pair.at[:, low, right], corners.at[1], sems, 5, -1, 1),
        send(pair.at[:, high, left], corners.at[2], sems, 6, 1, -1),
        send(pair.at[:, high, right], corners.at[3], sems, 7, 1, 1),
    ]


def lane_index(shape):
    return lax.broadcasted_iota(jnp.int32, shape, len(shape) - 1)


def row_index(shape):
    return lax.broadcasted_iota(jnp.int32, shape, len(shape) - 2)


def joined(which, pair, bands, sides, corners):
    def lanes(own, north, south):
        return jnp.concatenate(
            [own, jnp.where(lane_index(north.shape) < HALF, north, south)], axis=1
        )

    return jnp.concatenate(
        [
            lanes(pair[which], sides[0, which], sides[1, which]),
            lanes(bands[0, which], corners[0, which], corners[1, which]),
            lanes(bands[1, which], corners[2, which], corners[3, which]),
        ],
        axis=0,
    )


def after(field, axis):
    return pltpu.roll(field, field.shape[axis] - 1, axis)


def before(field, axis):
    return pltpu.roll(field, 1, axis)


def around_total(field):
    pair = after(field, 0) + before(field, 0)
    slanted = field + 0.5 * pair
    return pair + after(slanted, 1) + before(slanted, 1)


def inverse_of(value):
    near = pl.reciprocal(value, approx=True)
    return near * (2.0 - value * near)


def fill(k, packed, lane, side, shift):
    return jnp.where(lane == k, pltpu.roll(side, shift, 1), packed)


def by_level(levels, body, carry):
    def step(at, carry):
        for inner in range(GROUP):
            carry = body(at * GROUP + inner, carry)
        return carry

    return lax.fori_loop(0, levels // GROUP, step, carry)


def columns_kernel(
    temp_hbm,
    speed_hbm,
    mix_hbm,
    sea_hbm,
    tally_hbm,
    rain_hbm,
    temp_out,
    speed_out,
    root_out,
    ratio_out,
    scaled_out,
    temp,
    east,
    north,
    mix,
    value,
    factor,
    scale,
    coupling,
    sea,
    tally,
    depth,
    depth_e,
    depth_n,
    surf,
    totals,
    tail_ref,
    row_east,
    row_west,
    from_west,
    from_east,
    col_north,
    col_south,
    from_south,
    from_north,
    press_row,
    press_from_east,
    press_col,
    press_from_north,
    fix_row,
    fix_col,
    load_sems,
    edge_sems,
    bands,
    sides,
    corners,
    halo_sems,
    total_bands,
    total_sides,
    total_corners,
    total_sems,
):
    levels, rows, cols = temp.shape
    strips = rows // BAND
    greet_neighbours()
    pairs = [
        (sea_hbm, sea),
        (tally_hbm, tally),
        (rain_hbm, surf.at[1]),
        (temp_hbm, temp),
        (speed_hbm.at[0], east),
        (speed_hbm.at[1], north),
        (mix_hbm, mix),
    ]
    loads = [
        pltpu.make_async_copy(src, dst, load_sems.at[at]) for at, (src, dst) in enumerate(pairs)
    ]
    for copy in loads:
        copy.start()
    for copy in loads[:3]:
        copy.wait()

    tile = (rows, cols)
    latitude = lax.axis_index("gy") * cols + lane_index(tile)
    inner = (latitude > 0) & (latitude < cols * lax.axis_size("gy") - 1)
    wet_levels = jnp.where(inner & (sea[...] == 1), tally[...], 0).astype(F32)
    depth[...] = wet_levels
    surf[0] = wet_levels
    depth_e[...] = jnp.where(
        row_index(tile) == rows - 1, 0.0, jnp.minimum(wet_levels, after(wet_levels, 0))
    )
    depth_n[...] = jnp.where(
        lane_index(tile) == cols - 1, 0.0, jnp.minimum(wet_levels, after(wet_levels, 1))
    )

    lane = lane_index((rows, LANES))
    zero_side = jnp.zeros((rows, LANES), F32)
    low, high = slice(0, LANES), slice(cols - LANES, cols)
    def pack_temp(k, carry):
        to_north, to_south = carry
        one = pl.ds(k, 1)
        row_east[0, one, :] = temp[k, rows - 1 : rows, :]
        row_west[one, :] = temp[k, 0:1, :]
        to_north = fill(k, to_north, lane, temp[k, :, high], k + 1)
        to_south = fill(k, to_south, lane, temp[k, :, low], k)
        return to_north, to_south

    def pack_speed(k, to_north):
        row_east[1, pl.ds(k, 1), :] = east[k, rows - 1 : rows, :]
        return fill(k + HALF, to_north, lane, north[k, :, high], k + 1 + HALF)

    loads[3].wait()
    to_north, to_south = by_level(levels, pack_temp, (zero_side, zero_side))
    col_south[...] = to_south
    meet_neighbours()
    surf_copies = start_halo(surf, bands, sides, corners, halo_sems)
    edges = [
        send(row_west, from_east, edge_sems, 0, -1, 0),
        send(col_south, from_north, edge_sems, 1, 0, -1),
    ]
    loads[4].wait()
    loads[5].wait()
    col_north[...] = by_level(levels, pack_speed, to_north)
    edges += [
        send(row_east, from_west, edge_sems, 2, 1, 0),
        send(col_north, from_south, edge_sems, 3, 0, 1),
    ]

    loads[6].wait()

    band = (BAND, cols)
    band_row = row_index(band)

    def upwind(open_depth, level, speed, here, there):
        flux = speed * jnp.where(speed > 0.0, here, there)
        return jnp.where(level < open_depth, flux, 0.0)

    part = [pl.ds(at * BAND, BAND) for at in range(strips)]

    def assemble(k, carry):
        level = jnp.asarray(k, F32)
        later_level = jnp.minimum(k + 1, levels - 1)
        result = []
        previous = jnp.zeros(band, F32)
        here = temp[k, part[0], :]
        turned = pltpu.roll(here, BAND - 1, 0)
        for at in range(strips):
            above, keep = carry[at]
            if at + 1 < strips:
                later = temp[k, part[at + 1], :]
                later_turned = pltpu.roll(later, BAND - 1, 0)
                there = jnp.where(band_row == BAND - 1, later_turned, turned)
            else:
                there = turned
            flux = upwind(depth_e[part[at], :], level, east[k, part[at], :], here, there)
            turned_flux = pltpu.roll(flux, 1, 0)
            total = flux - jnp.where(band_row == 0, previous, turned_flux)
            previous = turned_flux
            flux = upwind(
                depth_n[part[at], :], level, north[k, part[at], :], here, after(here, 1)
            )
            total = total + (flux - before(flux, 1))
            value[k, part[at], :] = here - advect_scale * total
            coupling[k, part[at], :] = above
            below = jnp.where(
                level + 1.0 < depth[part[at], :], mix[later_level, part[at], :], 0.0
            )
            inverse_pivot = inverse_of((1.0 + below) + above * keep)
            scale[k, part[at], :] = inverse_pivot
            leading = below * inverse_pivot
            factor[k, part[at], :] = leading
            result.append((below, 1.0 - leading))
            if at + 1 < strips:
                here, turned = later, later_turned
        return tuple(result)

    nothing = jnp.zeros(band, F32)
    lax.fori_loop(0, levels, assemble, ((nothing, nothing),) * strips)

    for copy in surf_copies:
        copy.wait()
    wide = joined(0, surf, bands, sides, corners)
    last_e = jnp.minimum(wide[rows - 1 : rows, :cols], wide[rows : rows + 1, :cols])
    last_n = jnp.minimum(wide[:rows, cols - 1 : cols], wide[:rows, cols : cols + 1])
    open_w = jnp.minimum(wide[0:1, :cols], wide[-1:, :cols])
    open_s = jnp.minimum(wide[:rows, 0:1], wide[:rows, -1:])

    for copy in edges:
        copy.wait()
    level_row = row_index((levels, cols)).astype(F32)
    level_lane = lane.astype(F32)
    flux_w = upwind(open_w, level_row, from_west[1], from_west[0], row_west[...])
    flux_e = upwind(last_e, level_row, row_east[1], row_east[0], from_east[...])
    flux_s = upwind(
        open_s, level_lane, pltpu.roll(from_south[...], HALF, 1), from_south[...], col_south[...]
    )
    flux_n = upwind(
        last_n, level_lane, pltpu.roll(col_north[...], HALF, 1), col_north[...], from_north[...]
    )
    from_west[0] = advect_scale * flux_w
    from_west[1] = advect_scale * flux_e
    from_south[...] = advect_scale * flux_s
    from_north[...] = advect_scale * flux_n

    middle = [jnp.zeros((rows, cols - 2 * LANES), F32)] if cols > 2 * LANES else []

    def forward(k, x):
        one = pl.ds(k, 1)
        rim = jnp.concatenate(
            [
                jnp.where(lane == 0, pltpu.roll(from_south[...], LANES - k, 1), 0.0),
                *middle,
                jnp.where(
                    lane == LANES - 1, -pltpu.roll(from_north[...], LANES - 1 - k, 1), 0.0
                ),
            ],
            axis=1,
        )
        source = value[k] + rim
        source = jnp.concatenate(
            [
                source[:BAND] + jnp.where(band_row == 0, from_west[0, one, :], 0.0),
                source[BAND : rows - BAND],
                source[rows - BAND :]
                - jnp.where(band_row == BAND - 1, from_west[1, one, :], 0.0),
            ],
            axis=0,
        )
        x = (source + coupling[k] * x) * scale[k]
        temp[k] = x
        return x

    by_level(levels, forward, jnp.zeros(tile, F32))

    slope = force_scale / levels

    def backward(step, carry):
        x, tail = carry
        k = levels - 1 - step
        x = temp[k] + factor[k] * x
        temp_out[k] = x
        share = slope * x
        tail = tail + share
        value[k] = tail - 0.5 * share
        return x, tail

    x, tail = by_level(levels, backward, (jnp.zeros(tile, F32), jnp.zeros(tile, F32)))
    tail_ref[...] = tail

    def pack_press(k, carry):
        to_north, to_south = carry
        one = pl.ds(k, 1)
        press_row[0, one, :] = value[k, 0:1, :]
        press_row[1, one, :] = value[k, rows - 1 : rows, :]
        to_north = fill(k, to_north, lane, value[k, :, high], k + 1)
        to_south = fill(k, to_south, lane, value[k, :, low], k)
        return to_north, to_south

    to_north, to_south = by_level(levels, pack_press, (zero_side, zero_side))
    press_row[0] -= tail[0:1, :]
    press_row[1] -= tail[rows - 1 : rows, :]
    press_col[0] = to_south - tail[:, 0:1]
    press_col[1] = to_north - tail[:, cols - 1 : cols]
    press = [
        send(press_row.at[0], press_from_east, edge_sems, 4, -1, 0),
        send(press_col.at[0], press_from_north, edge_sems, 5, 0, -1),
    ]

    totals[...] = jnp.zeros(totals.shape, F32)

    def momentum(k, carry):
        level = jnp.asarray(k, F32)
        here = value[k, part[0], :] - tail_ref[part[0], :]
        turned = pltpu.roll(here, BAND - 1, 0)
        for at in range(strips):
            if at + 1 < strips:
                later = value[k, part[at + 1], :] - tail_ref[part[at + 1], :]
                later_turned = pltpu.roll(later, BAND - 1, 0)
                there = jnp.where(band_row == BAND - 1, later_turned, turned)
            else:
                there = turned
            speed = east[k, part[at], :] + (here - there)
            speed = jnp.where(level < depth_e[part[at], :], speed, 0.0)
            speed_out[0, k, part[at], :] = speed
            totals[0, part[at], :] += speed
            speed = north[k, part[at], :] + (here - after(here, 1))
            speed = jnp.where(level < depth_n[part[at], :], speed, 0.0)
            speed_out[1, k, part[at], :] = speed
            totals[1, part[at], :] += speed
            if at + 1 < strips:
                here, turned = later, later_turned
        return carry

    lax.fori_loop(0, levels, momentum, 0)

    for copy in press:
        copy.wait()
    speed_e = row_east[1] + (press_row[1] - press_from_east[...])
    speed_e = jnp.where(level_row < last_e, speed_e, 0.0)
    speed_n = pltpu.roll(col_north[...], HALF, 1) + (press_col[1] - press_from_north[...])
    speed_n = jnp.where(level_lane < last_n, speed_n, 0.0)
    fix_row[...] = speed_e
    fix_col[...] = speed_n
    totals[0, rows - 1 : rows, :] = jnp.sum(speed_e, axis=0, keepdims=True)
    totals[1, :, high] += jnp.where(
        lane == LANES - 1, jnp.sum(speed_n, axis=1, keepdims=True), 0.0
    )
    total_copies = start_halo(totals, total_bands, total_sides, total_corners, total_sems)

    def add_last(k, carry):
        speed_out[0, k, rows - 1 : rows, :] = fix_row[pl.ds(k, 1), :]
        speed_out[1, k, :, high] += jnp.where(
            lane == LANES - 1, pltpu.roll(fix_col[...], LANES - 1 - k, 1), 0.0
        )
        return carry

    by_level(levels, add_last, 0)

    source = source_scale * joined(1, surf, bands, sides, corners)
    root = jnp.sqrt(wide / levels)
    inverse = 1.0 / (damping + root * around_total(root))
    root_out[...] = root
    ratio_out[...] = root * inverse

    for copy in total_copies:
        copy.wait()
    total_e = joined(0, totals, total_bands, total_sides, total_corners)
    total_n = joined(1, totals, total_bands, total_sides, total_corners)
    divergence = total_e - before(total_e, 0) + total_n - before(total_n, 1)
    forcing = source - (divergence_scale / levels) * divergence
    scaled_out[...] = jnp.where(root > 0.0, forcing * inverse, 0.0)


def surface_kernel(
    temp_in, speed_in, root_in, ratio_in, scaled_in, temp_out, speed_out, out, sems
):
    rows, cols = out.shape
    copies = [
        pltpu.make_async_copy(temp_in, temp_out, sems.at[0]),
        pltpu.make_async_copy(speed_in.at[0], speed_out.at[0], sems.at[1]),
        pltpu.make_async_copy(speed_in.at[1], speed_out.at[1], sems.at[2]),
    ]
    for copy in copies:
        copy.start()
    root = root_in[...]
    ratio = ratio_in[...]
    scaled = scaled_in[...]
    update = scaled * (1.0 / cheb_gamma)
    iterate = update
    omega = 2.0 / cheb_gamma
    for _ in range(1, ITERS):
        omega = 1.0 / (cheb_gamma - omega / (4.0 * cheb_alpha * cheb_alpha))
        residual = scaled - iterate + ratio * around_total(root * iterate)
        update = omega * residual + (cheb_gamma * omega - 1.0) * update
        iterate = iterate + update
    out[...] = iterate[:rows, :cols]
    for copy in copies:
        copy.wait()


def local(temp, speeds, mix, sea, tally, rain):
    levels, rows, cols = temp.shape
    wide = pltpu.VMEM((rows + 2 * BAND, cols + LANES), F32)
    vmem = pl.BlockSpec(memory_space=pltpu.VMEM)
    field = pltpu.VMEM((levels, rows, cols), F32)
    plane = pltpu.VMEM((rows, cols), F32)
    plane_int = pltpu.VMEM((rows, cols), jnp.int32)
    two_planes = pltpu.VMEM((2, rows, cols), F32)
    row_set = pltpu.VMEM((levels, cols), F32)
    row_sets = pltpu.VMEM((2, levels, cols), F32)
    col_set = pltpu.VMEM((rows, LANES), F32)
    col_sets = pltpu.VMEM((2, rows, LANES), F32)
    inputs = [
        pltpu.with_memory_space_constraint(array, pltpu.HBM)
        for array in (temp, speeds, mix, sea, tally, rain)
    ]
    temp_next, speed_next, root, ratio, scaled = pl.pallas_call(
        columns_kernel,
        out_shape=[field, pltpu.VMEM((2, levels, rows, cols), F32), wide, wide, wide],
        in_specs=[pl.BlockSpec(memory_space=pltpu.HBM)] * 6,
        out_specs=[vmem] * 5,
        scratch_shapes=[field] * 8
        + [plane_int] * 2
        + [plane] * 3
        + [two_planes, two_planes, plane]
        + [row_sets, row_set, row_sets, row_set]
        + [col_set] * 4
        + [row_sets, row_set, col_sets, col_set]
        + [row_set, col_set]
        + [pltpu.SemaphoreType.DMA((7,)), pltpu.SemaphoreType.DMA((2, 6))]
        + halo_shapes(rows, cols) * 2,
        compiler_params=pltpu.CompilerParams(
            collective_id=0, has_side_effects=True, vmem_limit_bytes=48 * 2**20
        ),
        name="columns",
    )(*inputs)
    held = [
        pltpu.with_memory_space_constraint(array, pltpu.VMEM)
        for array in (temp_next, speed_next, root, ratio, scaled)
    ]
    return pl.pallas_call(
        surface_kernel,
        out_shape=[
            jax.ShapeDtypeStruct(temp.shape, F32),
            jax.ShapeDtypeStruct(speeds.shape, F32),
            jax.ShapeDtypeStruct((rows, cols), F32),
        ],
        in_specs=[vmem] * 5,
        out_specs=[pl.BlockSpec(memory_space=pltpu.HBM)] * 2 + [vmem],
        scratch_shapes=[pltpu.SemaphoreType.DMA((3,))],
        compiler_params=pltpu.CompilerParams(vmem_limit_bytes=32 * 2**20),
        name="surface",
    )(*held)


def solution(mesh):
    tile = P("gx", "gy")
    column = P(None, "gx", "gy")
    pair = P(None, None, "gx", "gy")
    return jax.shard_map(
        local,
        mesh=mesh,
        in_specs=(column, pair, column, tile, tile, tile),
        out_specs=(column, pair, tile),
        check_vma=False,
    )
```

```python
import jax
import jax.numpy as jnp
from jax import lax
from jax.experimental import pallas as pl
from jax.experimental.pallas import tpu as pltpu
from jax.sharding import PartitionSpec as P

ITERS = 6
damping = 0.05
lower_bound = 0.02
upper_bound = 2.0
cheb_alpha = 2.0 / (upper_bound - lower_bound)
cheb_gamma = (upper_bound + lower_bound) / 2.0
advect_scale = 0.4
force_scale = 4.0
source_scale = 0.5
divergence_scale = 4.0

MESH = pl.DeviceIdType.MESH
LANES = 128
HALF = LANES // 2
GROUP = 8
BAND = 8
F32 = jnp.float32
AROUND = ((1, 0), (-1, 0), (0, 1), (0, -1), (1, 1), (1, -1), (-1, 1), (-1, -1))


def device_at(dx, dy):
    nx, ny = lax.axis_size("gx"), lax.axis_size("gy")
    return (
        lax.rem(lax.axis_index("gx") + (dx + nx), nx),
        lax.rem(lax.axis_index("gy") + (dy + ny), ny),
    )


def greet_neighbours():
    for dx, dy in AROUND:
        pl.semaphore_signal(
            pltpu.get_barrier_semaphore(),
            inc=1,
            device_id=device_at(dx, dy),
            device_id_type=MESH,
        )


def meet_neighbours():
    pl.semaphore_wait(pltpu.get_barrier_semaphore(), len(AROUND))


def send(src, dst, sems, at, dx, dy):
    copy = pltpu.make_async_remote_copy(
        src_ref=src,
        dst_ref=dst,
        send_sem=sems.at[0, at],
        recv_sem=sems.at[1, at],
        device_id=device_at(dx, dy),
        device_id_type=MESH,
    )
    copy.start()
    return copy


def halo_shapes(rows, cols):
    return [
        pltpu.VMEM((2, 2, BAND, cols), F32),
        pltpu.VMEM((2, 2, rows, LANES), F32),
        pltpu.VMEM((4, 2, BAND, LANES), F32),
        pltpu.SemaphoreType.DMA((2, 8)),
    ]


def start_halo(pair, bands, sides, corners, sems):
    rows, cols = pair.shape[1:]
    low, high = pl.ds(0, BAND), pl.ds(rows - BAND, BAND)
    left, right = pl.ds(0, LANES), pl.ds(cols - LANES, LANES)
    return [
        send(pair.at[:, low, :], bands.at[0], sems, 0, -1, 0),
        send(pair.at[:, high, :], bands.at[1], sems, 1, 1, 0),
        send(pair.at[:, :, left], sides.at[0], sems, 2, 0, -1),
        send(pair.at[:, :, right], sides.at[1], sems, 3, 0, 1),
        send(pair.at[:, low, left], corners.at[0], sems, 4, -1, -1),
        send(pair.at[:, low, right], corners.at[1], sems, 5, -1, 1),
        send(pair.at[:, high, left], corners.at[2], sems, 6, 1, -1),
        send(pair.at[:, high, right], corners.at[3], sems, 7, 1, 1),
    ]


def lane_index(shape):
    return lax.broadcasted_iota(jnp.int32, shape, len(shape) - 1)


def row_index(shape):
    return lax.broadcasted_iota(jnp.int32, shape, len(shape) - 2)


def joined(which, pair, bands, sides, corners):
    def lanes(own, north, south):
        return jnp.concatenate(
            [own, jnp.where(lane_index(north.shape) < HALF, north, south)], axis=1
        )

    return jnp.concatenate(
        [
            lanes(pair[which], sides[0, which], sides[1, which]),
            lanes(bands[0, which], corners[0, which], corners[1, which]),
            lanes(bands[1, which], corners[2, which], corners[3, which]),
        ],
        axis=0,
    )


def after(field, axis):
    return pltpu.roll(field, field.shape[axis] - 1, axis)


def before(field, axis):
    return pltpu.roll(field, 1, axis)


def around_total(field):
    pair = after(field, 0) + before(field, 0)
    slanted = field + 0.5 * pair
    return pair + after(slanted, 1) + before(slanted, 1)


def inverse_of(value):
    near = pl.reciprocal(value, approx=True)
    return near * (2.0 - value * near)


def fill(k, packed, lane, side, shift):
    return jnp.where(lane == k, pltpu.roll(side, shift, 1), packed)


def by_level(levels, body, carry):
    def step(at, carry):
        for inner in range(GROUP):
            carry = body(at * GROUP + inner, carry)
        return carry

    return lax.fori_loop(0, levels // GROUP, step, carry)


def columns_kernel(
    temp_hbm,
    speed_hbm,
    mix_hbm,
    sea_hbm,
    tally_hbm,
    rain_hbm,
    temp_out,
    speed_out,
    root_out,
    ratio_out,
    scaled_out,
    temp,
    east,
    north,
    mix,
    value,
    factor,
    scale,
    sea,
    tally,
    depth,
    depth_e,
    depth_n,
    surf,
    totals,
    tail_ref,
    row_east,
    row_west,
    from_west,
    from_east,
    col_north,
    col_south,
    from_south,
    from_north,
    press_row,
    press_from_east,
    press_col,
    press_from_north,
    fix_row,
    fix_col,
    load_sems,
    chunk_sems,
    edge_sems,
    bands,
    sides,
    corners,
    halo_sems,
    total_bands,
    total_sides,
    total_corners,
    total_sems,
):
    levels, rows, cols = temp.shape
    strips = rows // BAND
    greet_neighbours()
    low, high = slice(0, LANES), slice(cols - LANES, cols)
    last_rows, last_lanes = pl.ds(rows - BAND, BAND), pl.ds(cols - LANES, LANES)
    other_rows, other_lanes = pl.ds(0, rows - BAND), pl.ds(0, cols - LANES)
    first_loads = [
        pltpu.make_async_copy(src, dst, load_sems.at[at])
        for at, (src, dst) in enumerate(
            (
                (sea_hbm, sea),
                (tally_hbm, tally),
                (rain_hbm, surf.at[1]),
                (temp_hbm, temp),
                (speed_hbm.at[1, :, :, last_lanes], north.at[:, :, last_lanes]),
                (speed_hbm.at[0, :, last_rows, :], east.at[:, last_rows, :]),
            )
        )
    ]
    for copy in first_loads:
        copy.start()
    chunks = levels // GROUP

    def load_mix(at):
        span = pl.ds(at * GROUP, GROUP)
        return pltpu.make_async_copy(mix_hbm.at[span], mix.at[span], chunk_sems.at[0, at])

    def load_speeds(at):
        span = pl.ds(at * GROUP, GROUP)
        return [
            pltpu.make_async_copy(
                speed_hbm.at[0, span, other_rows, :],
                east.at[span, other_rows, :],
                chunk_sems.at[1, at],
            ),
            pltpu.make_async_copy(
                speed_hbm.at[1, span, :, other_lanes],
                north.at[span, :, other_lanes],
                chunk_sems.at[2, at],
            ),
        ]

    for at in range(chunks):
        for copy in (load_mix(at), *load_speeds(at)):
            copy.start()
    for copy in first_loads[:3]:
        copy.wait()

    tile = (rows, cols)
    latitude = lax.axis_index("gy") * cols + lane_index(tile)
    inner = (latitude > 0) & (latitude < cols * lax.axis_size("gy") - 1)
    wet_levels = jnp.where(inner & (sea[...] == 1), tally[...], 0).astype(F32)
    depth[...] = wet_levels
    surf[0] = wet_levels
    depth_e[...] = jnp.where(
        row_index(tile) == rows - 1, 0.0, jnp.minimum(wet_levels, after(wet_levels, 0))
    )
    depth_n[...] = jnp.where(
        lane_index(tile) == cols - 1, 0.0, jnp.minimum(wet_levels, after(wet_levels, 1))
    )

    lane = lane_index((rows, LANES))
    zero_side = jnp.zeros((rows, LANES), F32)
    def pack_temp(k, carry):
        to_north, to_south = carry
        one = pl.ds(k, 1)
        row_east[0, one, :] = temp[k, rows - 1 : rows, :]
        row_west[one, :] = temp[k, 0:1, :]
        to_north = fill(k, to_north, lane, temp[k, :, high], k + 1)
        to_south = fill(k, to_south, lane, temp[k, :, low], k)
        return to_north, to_south

    def pack_speed(k, to_north):
        row_east[1, pl.ds(k, 1), :] = east[k, rows - 1 : rows, :]
        return fill(k + HALF, to_north, lane, north[k, :, high], k + 1 + HALF)

    first_loads[3].wait()
    to_north, to_south = by_level(levels, pack_temp, (zero_side, zero_side))
    col_south[...] = to_south
    meet_neighbours()
    surf_copies = start_halo(surf, bands, sides, corners, halo_sems)
    edges = [
        send(row_west, from_east, edge_sems, 0, -1, 0),
        send(col_south, from_north, edge_sems, 1, 0, -1),
    ]
    first_loads[4].wait()
    first_loads[5].wait()
    col_north[...] = by_level(levels, pack_speed, to_north)
    edges += [
        send(row_east, from_west, edge_sems, 2, 1, 0),
        send(col_north, from_south, edge_sems, 3, 0, 1),
    ]

    band = (BAND, cols)
    band_row = row_index(band)

    def upwind(open_depth, level, speed, here, there):
        flux = speed * jnp.where(speed > 0.0, here, there)
        return jnp.where(level < open_depth, flux, 0.0)

    part = [pl.ds(at * BAND, BAND) for at in range(strips)]

    def assemble(k, carry):
        level = jnp.asarray(k, F32)
        later_level = jnp.minimum(k + 1, levels - 1)
        result = []
        previous = jnp.zeros(band, F32)
        here = temp[k, part[0], :]
        turned = pltpu.roll(here, BAND - 1, 0)
        for at in range(strips):
            keep = carry[at]
            above = jnp.where(level < depth[part[at], :], mix[k, part[at], :], 0.0)
            if at + 1 < strips:
                later = temp[k, part[at + 1], :]
                later_turned = pltpu.roll(later, BAND - 1, 0)
                there = jnp.where(band_row == BAND - 1, later_turned, turned)
            else:
                there = turned
            flux = upwind(depth_e[part[at], :], level, east[k, part[at], :], here, there)
            turned_flux = pltpu.roll(flux, 1, 0)
            total = flux - jnp.where(band_row == 0, previous, turned_flux)
            previous = turned_flux
            flux = upwind(
                depth_n[part[at], :], level, north[k, part[at], :], here, after(here, 1)
            )
            total = total + (flux - before(flux, 1))
            value[k, part[at], :] = here - advect_scale * total
            below = jnp.where(
                level + 1.0 < depth[part[at], :], mix[later_level, part[at], :], 0.0
            )
            inverse_pivot = inverse_of((1.0 + below) + above * keep)
            scale[k, part[at], :] = inverse_pivot
            leading = below * inverse_pivot
            factor[k, part[at], :] = leading
            result.append(1.0 - leading)
            if at + 1 < strips:
                here, turned = later, later_turned
        return tuple(result)

    def assemble_chunk(at, carry):
        @pl.when(at + 1 < chunks)
        def _():
            load_mix(at + 1).wait()

        for copy in load_speeds(at):
            copy.wait()

        def step(half, carry):
            k = at * GROUP + 2 * half
            return assemble(k + 1, assemble(k, carry))

        return lax.fori_loop(0, GROUP // 2, step, carry)

    load_mix(0).wait()
    lax.fori_loop(0, chunks, assemble_chunk, (jnp.zeros(band, F32),) * strips)

    for copy in surf_copies:
        copy.wait()
    wide = joined(0, surf, bands, sides, corners)
    last_e = jnp.minimum(wide[rows - 1 : rows, :cols], wide[rows : rows + 1, :cols])
    last_n = jnp.minimum(wide[:rows, cols - 1 : cols], wide[:rows, cols : cols + 1])
    open_w = jnp.minimum(wide[0:1, :cols], wide[-1:, :cols])
    open_s = jnp.minimum(wide[:rows, 0:1], wide[:rows, -1:])

    for copy in edges:
        copy.wait()
    level_row = row_index((levels, cols)).astype(F32)
    level_lane = lane.astype(F32)
    flux_w = upwind(open_w, level_row, from_west[1], from_west[0], row_west[...])
    flux_e = upwind(last_e, level_row, row_east[1], row_east[0], from_east[...])
    flux_s = upwind(
        open_s, level_lane, pltpu.roll(from_south[...], HALF, 1), from_south[...], col_south[...]
    )
    flux_n = upwind(
        last_n, level_lane, pltpu.roll(col_north[...], HALF, 1), col_north[...], from_north[...]
    )
    from_west[0] = advect_scale * flux_w
    from_west[1] = advect_scale * flux_e
    from_south[...] = advect_scale * flux_s
    from_north[...] = advect_scale * flux_n

    middle = [jnp.zeros((rows, cols - 2 * LANES), F32)] if cols > 2 * LANES else []

    def forward(k, x):
        one = pl.ds(k, 1)
        rim = jnp.concatenate(
            [
                jnp.where(lane == 0, pltpu.roll(from_south[...], LANES - k, 1), 0.0),
                *middle,
                jnp.where(
                    lane == LANES - 1, -pltpu.roll(from_north[...], LANES - 1 - k, 1), 0.0
                ),
            ],
            axis=1,
        )
        source = value[k] + rim
        source = jnp.concatenate(
            [
                source[:BAND] + jnp.where(band_row == 0, from_west[0, one, :], 0.0),
                source[BAND : rows - BAND],
                source[rows - BAND :]
                - jnp.where(band_row == BAND - 1, from_west[1, one, :], 0.0),
            ],
            axis=0,
        )
        above = jnp.where(jnp.asarray(k, F32) < depth[...], mix[k], 0.0)
        x = (source + above * x) * scale[k]
        temp[k] = x
        return x

    by_level(levels, forward, jnp.zeros(tile, F32))

    slope = force_scale / levels

    def backward(step, carry):
        x, tail, to_north, to_south = carry
        k = levels - 1 - step
        one = pl.ds(k, 1)
        x = temp[k] + factor[k] * x
        temp_out[k] = x
        share = slope * x
        tail = tail + share
        press = tail - 0.5 * share
        value[k] = press
        press_row[0, one, :] = press[0:1, :]
        press_row[1, one, :] = press[rows - 1 : rows, :]
        to_north = fill(k, to_north, lane, press[:, high], k + 1)
        to_south = fill(k, to_south, lane, press[:, low], k)
        return x, tail, to_north, to_south

    zero_tile = jnp.zeros(tile, F32)
    x, tail, to_north, to_south = by_level(
        levels, backward, (zero_tile, zero_tile, zero_side, zero_side)
    )
    tail_ref[...] = tail
    press_row[0] -= tail[0:1, :]
    press_row[1] -= tail[rows - 1 : rows, :]
    press_col[0] = to_south - tail[:, 0:1]
    press_col[1] = to_north - tail[:, cols - 1 : cols]
    press = [
        send(press_row.at[0], press_from_east, edge_sems, 4, -1, 0),
        send(press_col.at[0], press_from_north, edge_sems, 5, 0, -1),
    ]

    totals[...] = jnp.zeros(totals.shape, F32)

    def momentum(k, carry):
        level = jnp.asarray(k, F32)
        here = value[k, part[0], :] - tail_ref[part[0], :]
        turned = pltpu.roll(here, BAND - 1, 0)
        for at in range(strips):
            if at + 1 < strips:
                later = value[k, part[at + 1], :] - tail_ref[part[at + 1], :]
                later_turned = pltpu.roll(later, BAND - 1, 0)
                there = jnp.where(band_row == BAND - 1, later_turned, turned)
            else:
                there = turned
            speed = east[k, part[at], :] + (here - there)
            speed = jnp.where(level < depth_e[part[at], :], speed, 0.0)
            speed_out[0, k, part[at], :] = speed
            totals[0, part[at], :] += speed
            speed = north[k, part[at], :] + (here - after(here, 1))
            speed = jnp.where(level < depth_n[part[at], :], speed, 0.0)
            speed_out[1, k, part[at], :] = speed
            totals[1, part[at], :] += speed
            if at + 1 < strips:
                here, turned = later, later_turned
        return carry

    lax.fori_loop(0, levels, momentum, 0)

    for copy in press:
        copy.wait()
    speed_e = row_east[1] + (press_row[1] - press_from_east[...])
    speed_e = jnp.where(level_row < last_e, speed_e, 0.0)
    speed_n = pltpu.roll(col_north[...], HALF, 1) + (press_col[1] - press_from_north[...])
    speed_n = jnp.where(level_lane < last_n, speed_n, 0.0)
    fix_row[...] = speed_e
    fix_col[...] = speed_n
    totals[0, rows - 1 : rows, :] = jnp.sum(speed_e, axis=0, keepdims=True)
    totals[1, :, high] += jnp.where(
        lane == LANES - 1, jnp.sum(speed_n, axis=1, keepdims=True), 0.0
    )
    total_copies = start_halo(totals, total_bands, total_sides, total_corners, total_sems)

    def add_last(k, carry):
        speed_out[0, k, rows - 1 : rows, :] = fix_row[pl.ds(k, 1), :]
        speed_out[1, k, :, high] += jnp.where(
            lane == LANES - 1, pltpu.roll(fix_col[...], LANES - 1 - k, 1), 0.0
        )
        return carry

    by_level(levels, add_last, 0)

    source = source_scale * joined(1, surf, bands, sides, corners)
    root = jnp.sqrt(wide / levels)
    inverse = 1.0 / (damping + root * around_total(root))
    root_out[...] = root
    ratio_out[...] = root * inverse

    for copy in total_copies:
        copy.wait()
    total_e = joined(0, totals, total_bands, total_sides, total_corners)
    total_n = joined(1, totals, total_bands, total_sides, total_corners)
    divergence = total_e - before(total_e, 0) + total_n - before(total_n, 1)
    forcing = source - (divergence_scale / levels) * divergence
    scaled_out[...] = jnp.where(root > 0.0, forcing * inverse, 0.0)


def surface_kernel(
    temp_in, speed_in, root_in, ratio_in, scaled_in, temp_out, speed_out, out, sems
):
    rows, cols = out.shape
    copies = [
        pltpu.make_async_copy(temp_in, temp_out, sems.at[0]),
        pltpu.make_async_copy(speed_in.at[0], speed_out.at[0], sems.at[1]),
        pltpu.make_async_copy(speed_in.at[1], speed_out.at[1], sems.at[2]),
    ]
    for copy in copies:
        copy.start()
    root = root_in[...]
    ratio = ratio_in[...]
    scaled = scaled_in[...]
    update = scaled * (1.0 / cheb_gamma)
    iterate = update
    omega = 2.0 / cheb_gamma
    for _ in range(1, ITERS):
        omega = 1.0 / (cheb_gamma - omega / (4.0 * cheb_alpha * cheb_alpha))
        residual = scaled - iterate + ratio * around_total(root * iterate)
        update = omega * residual + (cheb_gamma * omega - 1.0) * update
        iterate = iterate + update
    out[...] = iterate[:rows, :cols]
    for copy in copies:
        copy.wait()


def local(temp, speeds, mix, sea, tally, rain):
    levels, rows, cols = temp.shape
    wide = pltpu.VMEM((rows + 2 * BAND, cols + LANES), F32)
    vmem = pl.BlockSpec(memory_space=pltpu.VMEM)
    field = pltpu.VMEM((levels, rows, cols), F32)
    plane = pltpu.VMEM((rows, cols), F32)
    plane_int = pltpu.VMEM((rows, cols), jnp.int32)
    two_planes = pltpu.VMEM((2, rows, cols), F32)
    row_set = pltpu.VMEM((levels, cols), F32)
    row_sets = pltpu.VMEM((2, levels, cols), F32)
    col_set = pltpu.VMEM((rows, LANES), F32)
    col_sets = pltpu.VMEM((2, rows, LANES), F32)
    inputs = [
        pltpu.with_memory_space_constraint(array, pltpu.HBM)
        for array in (temp, speeds, mix, sea, tally, rain)
    ]
    temp_next, speed_next, root, ratio, scaled = pl.pallas_call(
        columns_kernel,
        out_shape=[field, pltpu.VMEM((2, levels, rows, cols), F32), wide, wide, wide],
        in_specs=[pl.BlockSpec(memory_space=pltpu.HBM)] * 6,
        out_specs=[vmem] * 5,
        scratch_shapes=[field] * 7
        + [plane_int] * 2
        + [plane] * 3
        + [two_planes, two_planes, plane]
        + [row_sets, row_set, row_sets, row_set]
        + [col_set] * 4
        + [row_sets, row_set, col_sets, col_set]
        + [row_set, col_set]
        + [
            pltpu.SemaphoreType.DMA((6,)),
            pltpu.SemaphoreType.DMA((3, levels // GROUP)),
            pltpu.SemaphoreType.DMA((2, 6)),
        ]
        + halo_shapes(rows, cols) * 2,
        compiler_params=pltpu.CompilerParams(
            collective_id=0, has_side_effects=True, vmem_limit_bytes=48 * 2**20
        ),
        name="columns",
    )(*inputs)
    held = [
        pltpu.with_memory_space_constraint(array, pltpu.VMEM)
        for array in (temp_next, speed_next, root, ratio, scaled)
    ]
    return pl.pallas_call(
        surface_kernel,
        out_shape=[
            jax.ShapeDtypeStruct(temp.shape, F32),
            jax.ShapeDtypeStruct(speeds.shape, F32),
            jax.ShapeDtypeStruct((rows, cols), F32),
        ],
        in_specs=[vmem] * 5,
        out_specs=[pl.BlockSpec(memory_space=pltpu.HBM)] * 2 + [vmem],
        scratch_shapes=[pltpu.SemaphoreType.DMA((3,))],
        compiler_params=pltpu.CompilerParams(vmem_limit_bytes=32 * 2**20),
        name="surface",
    )(*held)


def solution(mesh):
    tile = P("gx", "gy")
    column = P(None, "gx", "gy")
    pair = P(None, None, "gx", "gy")
    return jax.shard_map(
        local,
        mesh=mesh,
        in_specs=(column, pair, column, tile, tile, tile),
        out_specs=(column, pair, tile),
        check_vma=False,
    )
```

```python
import jax
import jax.numpy as jnp
from jax import lax
from jax.experimental import pallas as pl
from jax.experimental.pallas import tpu as pltpu
from jax.sharding import PartitionSpec as P

ITERS = 6
damping = 0.05
lower_bound = 0.02
upper_bound = 2.0
cheb_alpha = 2.0 / (upper_bound - lower_bound)
cheb_gamma = (upper_bound + lower_bound) / 2.0
advect_scale = 0.4
force_scale = 4.0
source_scale = 0.5
divergence_scale = 4.0

MESH = pl.DeviceIdType.MESH
LANES = 128
HALF = LANES // 2
GROUP = 8
BAND = 8
F32 = jnp.float32
AROUND = ((1, 0), (-1, 0), (0, 1), (0, -1), (1, 1), (1, -1), (-1, 1), (-1, -1))


def device_at(dx, dy):
    nx, ny = lax.axis_size("gx"), lax.axis_size("gy")
    return (
        lax.rem(lax.axis_index("gx") + (dx + nx), nx),
        lax.rem(lax.axis_index("gy") + (dy + ny), ny),
    )


def greet_neighbours():
    for dx, dy in AROUND:
        pl.semaphore_signal(
            pltpu.get_barrier_semaphore(),
            inc=1,
            device_id=device_at(dx, dy),
            device_id_type=MESH,
        )


def meet_neighbours():
    pl.semaphore_wait(pltpu.get_barrier_semaphore(), len(AROUND))


def send(src, dst, sems, at, dx, dy):
    copy = pltpu.make_async_remote_copy(
        src_ref=src,
        dst_ref=dst,
        send_sem=sems.at[0, at],
        recv_sem=sems.at[1, at],
        device_id=device_at(dx, dy),
        device_id_type=MESH,
    )
    copy.start()
    return copy


def halo_shapes(rows, cols):
    return [
        pltpu.VMEM((2, 2, BAND, cols), F32),
        pltpu.VMEM((2, 2, rows, LANES), F32),
        pltpu.VMEM((4, 2, BAND, LANES), F32),
        pltpu.SemaphoreType.DMA((2, 8)),
    ]


def start_halo(pair, bands, sides, corners, sems):
    rows, cols = pair.shape[1:]
    low, high = pl.ds(0, BAND), pl.ds(rows - BAND, BAND)
    left, right = pl.ds(0, LANES), pl.ds(cols - LANES, LANES)
    return [
        send(pair.at[:, low, :], bands.at[0], sems, 0, -1, 0),
        send(pair.at[:, high, :], bands.at[1], sems, 1, 1, 0),
        send(pair.at[:, :, left], sides.at[0], sems, 2, 0, -1),
        send(pair.at[:, :, right], sides.at[1], sems, 3, 0, 1),
        send(pair.at[:, low, left], corners.at[0], sems, 4, -1, -1),
        send(pair.at[:, low, right], corners.at[1], sems, 5, -1, 1),
        send(pair.at[:, high, left], corners.at[2], sems, 6, 1, -1),
        send(pair.at[:, high, right], corners.at[3], sems, 7, 1, 1),
    ]


def lane_index(shape):
    return lax.broadcasted_iota(jnp.int32, shape, len(shape) - 1)


def row_index(shape):
    return lax.broadcasted_iota(jnp.int32, shape, len(shape) - 2)


def joined(which, pair, bands, sides, corners):
    def lanes(own, north, south):
        return jnp.concatenate(
            [own, jnp.where(lane_index(north.shape) < HALF, north, south)], axis=1
        )

    return jnp.concatenate(
        [
            lanes(pair[which], sides[0, which], sides[1, which]),
            lanes(bands[0, which], corners[0, which], corners[1, which]),
            lanes(bands[1, which], corners[2, which], corners[3, which]),
        ],
        axis=0,
    )


def after(field, axis):
    return pltpu.roll(field, field.shape[axis] - 1, axis)


def before(field, axis):
    return pltpu.roll(field, 1, axis)


def around_total(field):
    pair = after(field, 0) + before(field, 0)
    slanted = field + 0.5 * pair
    return pair + after(slanted, 1) + before(slanted, 1)


def inverse_of(value):
    near = pl.reciprocal(value, approx=True)
    return near * (2.0 - value * near)


def fill(k, packed, lane, side, shift):
    return jnp.where(lane == k, pltpu.roll(side, shift, 1), packed)


def by_level(levels, body, carry):
    def step(at, carry):
        for inner in range(GROUP):
            carry = body(at * GROUP + inner, carry)
        return carry

    return lax.fori_loop(0, levels // GROUP, step, carry)


def columns_kernel(
    temp_hbm,
    speed_hbm,
    mix_hbm,
    sea_hbm,
    tally_hbm,
    rain_hbm,
    temp_out,
    speed_out,
    root_out,
    ratio_out,
    scaled_out,
    temp,
    east,
    north,
    mix,
    value,
    factor,
    scale,
    sea,
    tally,
    depth,
    depth_e,
    depth_n,
    surf,
    totals,
    tail_ref,
    row_east,
    row_west,
    from_west,
    from_east,
    col_north,
    col_south,
    from_south,
    from_north,
    press_row,
    press_from_east,
    press_col,
    press_from_north,
    fix_row,
    fix_col,
    load_sems,
    chunk_sems,
    edge_sems,
    bands,
    sides,
    corners,
    halo_sems,
    total_bands,
    total_sides,
    total_corners,
    total_sems,
):
    levels, rows, cols = temp.shape
    strips = rows // BAND
    greet_neighbours()
    low, high = slice(0, LANES), slice(cols - LANES, cols)
    first_loads = [
        pltpu.make_async_copy(src, dst, load_sems.at[at])
        for at, (src, dst) in enumerate(
            ((sea_hbm, sea), (tally_hbm, tally), (rain_hbm, surf.at[1]))
        )
    ]
    for copy in first_loads:
        copy.start()
    chunks = levels // GROUP

    def load_mix(at):
        span = pl.ds(at * GROUP, GROUP)
        return pltpu.make_async_copy(mix_hbm.at[span], mix.at[span], chunk_sems.at[0, at])

    def load_rest(at):
        span = pl.ds(at * GROUP, GROUP)
        return [
            pltpu.make_async_copy(temp_hbm.at[span], temp.at[span], chunk_sems.at[1, at]),
            pltpu.make_async_copy(speed_hbm.at[0, span], east.at[span], chunk_sems.at[2, at]),
            pltpu.make_async_copy(speed_hbm.at[1, span], north.at[span], chunk_sems.at[3, at]),
        ]

    load_mix(0).start()
    for at in range(chunks):
        for copy in load_rest(at):
            copy.start()
        if at + 1 < chunks:
            load_mix(at + 1).start()
    for copy in first_loads:
        copy.wait()

    tile = (rows, cols)
    latitude = lax.axis_index("gy") * cols + lane_index(tile)
    inner = (latitude > 0) & (latitude < cols * lax.axis_size("gy") - 1)
    wet_levels = jnp.where(inner & (sea[...] == 1), tally[...], 0).astype(F32)
    depth[...] = wet_levels
    surf[0] = wet_levels
    depth_e[...] = jnp.where(
        row_index(tile) == rows - 1, 0.0, jnp.minimum(wet_levels, after(wet_levels, 0))
    )
    depth_n[...] = jnp.where(
        lane_index(tile) == cols - 1, 0.0, jnp.minimum(wet_levels, after(wet_levels, 1))
    )

    lane = lane_index((rows, LANES))
    zero_side = jnp.zeros((rows, LANES), F32)
    band = (BAND, cols)
    band_row = row_index(band)

    def upwind(open_depth, level, speed, here, there):
        flux = speed * jnp.where(speed > 0.0, here, there)
        return jnp.where(level < open_depth, flux, 0.0)

    part = [pl.ds(at * BAND, BAND) for at in range(strips)]

    def assemble(k, carry):
        level = jnp.asarray(k, F32)
        later_level = jnp.minimum(k + 1, levels - 1)
        result = []
        previous = jnp.zeros(band, F32)
        here = temp[k, part[0], :]
        turned = pltpu.roll(here, BAND - 1, 0)
        for at in range(strips):
            keep = carry[at]
            above = jnp.where(level < depth[part[at], :], mix[k, part[at], :], 0.0)
            if at + 1 < strips:
                later = temp[k, part[at + 1], :]
                later_turned = pltpu.roll(later, BAND - 1, 0)
                there = jnp.where(band_row == BAND - 1, later_turned, turned)
            else:
                there = turned
            flux = upwind(depth_e[part[at], :], level, east[k, part[at], :], here, there)
            turned_flux = pltpu.roll(flux, 1, 0)
            total = flux - jnp.where(band_row == 0, previous, turned_flux)
            previous = turned_flux
            flux = upwind(
                depth_n[part[at], :], level, north[k, part[at], :], here, after(here, 1)
            )
            total = total + (flux - before(flux, 1))
            value[k, part[at], :] = here - advect_scale * total
            below = jnp.where(
                level + 1.0 < depth[part[at], :], mix[later_level, part[at], :], 0.0
            )
            inverse_pivot = inverse_of((1.0 + below) + above * keep)
            scale[k, part[at], :] = inverse_pivot
            leading = below * inverse_pivot
            factor[k, part[at], :] = leading
            result.append(1.0 - leading)
            if at + 1 < strips:
                here, turned = later, later_turned
        return tuple(result)

    def assemble_chunk(at, carry):
        @pl.when(at + 1 < chunks)
        def _():
            load_mix(at + 1).wait()

        def step(half, carry):
            k = at * GROUP + 2 * half
            return assemble(k + 1, assemble(k, carry))

        return lax.fori_loop(0, GROUP // 2, step, carry)

    def assemble_early(at, carry):
        for copy in load_rest(at):
            copy.wait()
        return assemble_chunk(at, carry)

    early = min(2, chunks)
    load_mix(0).wait()
    carry = lax.fori_loop(0, early, assemble_early, (jnp.zeros(band, F32),) * strips)
    for at in range(early, chunks):
        for copy in load_rest(at):
            copy.wait()

    def pack_temp(k, carry):
        to_north, to_south = carry
        one = pl.ds(k, 1)
        row_east[0, one, :] = temp[k, rows - 1 : rows, :]
        row_west[one, :] = temp[k, 0:1, :]
        to_north = fill(k, to_north, lane, temp[k, :, high], k + 1)
        to_south = fill(k, to_south, lane, temp[k, :, low], k)
        return to_north, to_south

    def pack_speed(k, to_north):
        row_east[1, pl.ds(k, 1), :] = east[k, rows - 1 : rows, :]
        return fill(k + HALF, to_north, lane, north[k, :, high], k + 1 + HALF)

    to_north, to_south = by_level(levels, pack_temp, (zero_side, zero_side))
    col_south[...] = to_south
    meet_neighbours()
    surf_copies = start_halo(surf, bands, sides, corners, halo_sems)
    edges = [
        send(row_west, from_east, edge_sems, 0, -1, 0),
        send(col_south, from_north, edge_sems, 1, 0, -1),
    ]
    col_north[...] = by_level(levels, pack_speed, to_north)
    edges += [
        send(row_east, from_west, edge_sems, 2, 1, 0),
        send(col_north, from_south, edge_sems, 3, 0, 1),
    ]

    lax.fori_loop(early, chunks, assemble_chunk, carry)

    for copy in surf_copies:
        copy.wait()
    wide = joined(0, surf, bands, sides, corners)
    last_e = jnp.minimum(wide[rows - 1 : rows, :cols], wide[rows : rows + 1, :cols])
    last_n = jnp.minimum(wide[:rows, cols - 1 : cols], wide[:rows, cols : cols + 1])
    open_w = jnp.minimum(wide[0:1, :cols], wide[-1:, :cols])
    open_s = jnp.minimum(wide[:rows, 0:1], wide[:rows, -1:])

    for copy in edges:
        copy.wait()
    level_row = row_index((levels, cols)).astype(F32)
    level_lane = lane.astype(F32)
    flux_w = upwind(open_w, level_row, from_west[1], from_west[0], row_west[...])
    flux_e = upwind(last_e, level_row, row_east[1], row_east[0], from_east[...])
    flux_s = upwind(
        open_s, level_lane, pltpu.roll(from_south[...], HALF, 1), from_south[...], col_south[...]
    )
    flux_n = upwind(
        last_n, level_lane, pltpu.roll(col_north[...], HALF, 1), col_north[...], from_north[...]
    )
    from_west[0] = advect_scale * flux_w
    from_west[1] = advect_scale * flux_e
    from_south[...] = advect_scale * flux_s
    from_north[...] = advect_scale * flux_n

    middle = [jnp.zeros((rows, cols - 2 * LANES), F32)] if cols > 2 * LANES else []

    def forward(k, x):
        one = pl.ds(k, 1)
        rim = jnp.concatenate(
            [
                jnp.where(lane == 0, pltpu.roll(from_south[...], LANES - k, 1), 0.0),
                *middle,
                jnp.where(
                    lane == LANES - 1, -pltpu.roll(from_north[...], LANES - 1 - k, 1), 0.0
                ),
            ],
            axis=1,
        )
        source = value[k] + rim
        source = jnp.concatenate(
            [
                source[:BAND] + jnp.where(band_row == 0, from_west[0, one, :], 0.0),
                source[BAND : rows - BAND],
                source[rows - BAND :]
                - jnp.where(band_row == BAND - 1, from_west[1, one, :], 0.0),
            ],
            axis=0,
        )
        above = jnp.where(jnp.asarray(k, F32) < depth[...], mix[k], 0.0)
        x = (source + above * x) * scale[k]
        temp[k] = x
        return x

    by_level(levels, forward, jnp.zeros(tile, F32))

    slope = force_scale / levels

    def backward(step, carry):
        x, tail, to_north, to_south = carry
        k = levels - 1 - step
        one = pl.ds(k, 1)
        x = temp[k] + factor[k] * x
        temp_out[k] = x
        share = slope * x
        tail = tail + share
        press = tail - 0.5 * share
        value[k] = press
        press_row[0, one, :] = press[0:1, :]
        press_row[1, one, :] = press[rows - 1 : rows, :]
        to_north = fill(k, to_north, lane, press[:, high], k + 1)
        to_south = fill(k, to_south, lane, press[:, low], k)
        return x, tail, to_north, to_south

    zero_tile = jnp.zeros(tile, F32)
    x, tail, to_north, to_south = by_level(
        levels, backward, (zero_tile, zero_tile, zero_side, zero_side)
    )
    tail_ref[...] = tail
    press_row[0] -= tail[0:1, :]
    press_row[1] -= tail[rows - 1 : rows, :]
    press_col[0] = to_south - tail[:, 0:1]
    press_col[1] = to_north - tail[:, cols - 1 : cols]
    press = [
        send(press_row.at[0], press_from_east, edge_sems, 4, -1, 0),
        send(press_col.at[0], press_from_north, edge_sems, 5, 0, -1),
    ]

    totals[...] = jnp.zeros(totals.shape, F32)

    def momentum(k, carry):
        level = jnp.asarray(k, F32)
        here = value[k, part[0], :] - tail_ref[part[0], :]
        turned = pltpu.roll(here, BAND - 1, 0)
        for at in range(strips):
            if at + 1 < strips:
                later = value[k, part[at + 1], :] - tail_ref[part[at + 1], :]
                later_turned = pltpu.roll(later, BAND - 1, 0)
                there = jnp.where(band_row == BAND - 1, later_turned, turned)
            else:
                there = turned
            speed = east[k, part[at], :] + (here - there)
            speed = jnp.where(level < depth_e[part[at], :], speed, 0.0)
            speed_out[0, k, part[at], :] = speed
            totals[0, part[at], :] += speed
            speed = north[k, part[at], :] + (here - after(here, 1))
            speed = jnp.where(level < depth_n[part[at], :], speed, 0.0)
            speed_out[1, k, part[at], :] = speed
            totals[1, part[at], :] += speed
            if at + 1 < strips:
                here, turned = later, later_turned
        return carry

    lax.fori_loop(0, levels, momentum, 0)

    for copy in press:
        copy.wait()
    speed_e = row_east[1] + (press_row[1] - press_from_east[...])
    speed_e = jnp.where(level_row < last_e, speed_e, 0.0)
    speed_n = pltpu.roll(col_north[...], HALF, 1) + (press_col[1] - press_from_north[...])
    speed_n = jnp.where(level_lane < last_n, speed_n, 0.0)
    fix_row[...] = speed_e
    fix_col[...] = speed_n
    totals[0, rows - 1 : rows, :] = jnp.sum(speed_e, axis=0, keepdims=True)
    totals[1, :, high] += jnp.where(
        lane == LANES - 1, jnp.sum(speed_n, axis=1, keepdims=True), 0.0
    )
    total_copies = start_halo(totals, total_bands, total_sides, total_corners, total_sems)

    def add_last(k, carry):
        speed_out[0, k, rows - 1 : rows, :] = fix_row[pl.ds(k, 1), :]
        speed_out[1, k, :, high] += jnp.where(
            lane == LANES - 1, pltpu.roll(fix_col[...], LANES - 1 - k, 1), 0.0
        )
        return carry

    by_level(levels, add_last, 0)

    source = source_scale * joined(1, surf, bands, sides, corners)
    root = jnp.sqrt(wide / levels)
    inverse = 1.0 / (damping + root * around_total(root))
    root_out[...] = root
    ratio_out[...] = root * inverse

    for copy in total_copies:
        copy.wait()
    total_e = joined(0, totals, total_bands, total_sides, total_corners)
    total_n = joined(1, totals, total_bands, total_sides, total_corners)
    divergence = total_e - before(total_e, 0) + total_n - before(total_n, 1)
    forcing = source - (divergence_scale / levels) * divergence
    scaled_out[...] = jnp.where(root > 0.0, forcing * inverse, 0.0)


def surface_kernel(
    temp_in, speed_in, root_in, ratio_in, scaled_in, temp_out, speed_out, out, sems
):
    rows, cols = out.shape
    pairs = [(temp_in, temp_out)] + [(speed_in.at[at], speed_out.at[at]) for at in range(2)]
    chunk = temp_in.shape[0] // sems.shape[1]
    copies = [
        pltpu.make_async_copy(
            src.at[pl.ds(at * chunk, chunk)], dst.at[pl.ds(at * chunk, chunk)], sems.at[which, at]
        )
        for at in range(sems.shape[1])
        for which, (src, dst) in enumerate(pairs)
    ]
    for copy in copies:
        copy.start()
    root = root_in[...]
    ratio = ratio_in[...]
    scaled = scaled_in[...]
    update = scaled * (1.0 / cheb_gamma)
    iterate = update
    omega = 2.0 / cheb_gamma
    for _ in range(1, ITERS):
        omega = 1.0 / (cheb_gamma - omega / (4.0 * cheb_alpha * cheb_alpha))
        residual = scaled - iterate + ratio * around_total(root * iterate)
        update = omega * residual + (cheb_gamma * omega - 1.0) * update
        iterate = iterate + update
    out[...] = iterate[:rows, :cols]
    for copy in copies:
        copy.wait()


def local(temp, speeds, mix, sea, tally, rain):
    levels, rows, cols = temp.shape
    wide = pltpu.VMEM((rows + 2 * BAND, cols + LANES), F32)
    vmem = pl.BlockSpec(memory_space=pltpu.VMEM)
    field = pltpu.VMEM((levels, rows, cols), F32)
    plane = pltpu.VMEM((rows, cols), F32)
    plane_int = pltpu.VMEM((rows, cols), jnp.int32)
    two_planes = pltpu.VMEM((2, rows, cols), F32)
    row_set = pltpu.VMEM((levels, cols), F32)
    row_sets = pltpu.VMEM((2, levels, cols), F32)
    col_set = pltpu.VMEM((rows, LANES), F32)
    col_sets = pltpu.VMEM((2, rows, LANES), F32)
    inputs = [
        pltpu.with_memory_space_constraint(array, pltpu.HBM)
        for array in (temp, speeds, mix, sea, tally, rain)
    ]
    temp_next, speed_next, root, ratio, scaled = pl.pallas_call(
        columns_kernel,
        out_shape=[field, pltpu.VMEM((2, levels, rows, cols), F32), wide, wide, wide],
        in_specs=[pl.BlockSpec(memory_space=pltpu.HBM)] * 6,
        out_specs=[vmem] * 5,
        scratch_shapes=[field] * 7
        + [plane_int] * 2
        + [plane] * 3
        + [two_planes, two_planes, plane]
        + [row_sets, row_set, row_sets, row_set]
        + [col_set] * 4
        + [row_sets, row_set, col_sets, col_set]
        + [row_set, col_set]
        + [
            pltpu.SemaphoreType.DMA((3,)),
            pltpu.SemaphoreType.DMA((4, levels // GROUP)),
            pltpu.SemaphoreType.DMA((2, 6)),
        ]
        + halo_shapes(rows, cols) * 2,
        compiler_params=pltpu.CompilerParams(
            collective_id=0, has_side_effects=True, vmem_limit_bytes=48 * 2**20
        ),
        name="columns",
    )(*inputs)
    held = [
        pltpu.with_memory_space_constraint(array, pltpu.VMEM)
        for array in (temp_next, speed_next, root, ratio, scaled)
    ]
    return pl.pallas_call(
        surface_kernel,
        out_shape=[
            jax.ShapeDtypeStruct(temp.shape, F32),
            jax.ShapeDtypeStruct(speeds.shape, F32),
            jax.ShapeDtypeStruct((rows, cols), F32),
        ],
        in_specs=[vmem] * 5,
        out_specs=[pl.BlockSpec(memory_space=pltpu.HBM)] * 2 + [vmem],
        scratch_shapes=[pltpu.SemaphoreType.DMA((3, levels // GROUP))],
        compiler_params=pltpu.CompilerParams(vmem_limit_bytes=32 * 2**20),
        name="surface",
    )(*held)


def solution(mesh):
    tile = P("gx", "gy")
    column = P(None, "gx", "gy")
    pair = P(None, None, "gx", "gy")
    return jax.shard_map(
        local,
        mesh=mesh,
        in_specs=(column, pair, column, tile, tile, tile),
        out_specs=(column, pair, tile),
        check_vma=False,
    )
```

```python
import jax
import jax.numpy as jnp
from jax import lax
from jax.experimental import pallas as pl
from jax.experimental.pallas import tpu as pltpu
from jax.sharding import PartitionSpec as P

ITERS = 6
damping = 0.05
lower_bound = 0.02
upper_bound = 2.0
cheb_alpha = 2.0 / (upper_bound - lower_bound)
cheb_gamma = (upper_bound + lower_bound) / 2.0
advect_scale = 0.4
force_scale = 4.0
source_scale = 0.5
divergence_scale = 4.0

MESH = pl.DeviceIdType.MESH
LANES = 128
HALF = LANES // 2
GROUP = 8
QUAD = 4
BAND = 8
F32 = jnp.float32
AROUND = ((1, 0), (-1, 0), (0, 1), (0, -1), (1, 1), (1, -1), (-1, 1), (-1, -1))


def device_at(dx, dy):
    nx, ny = lax.axis_size("gx"), lax.axis_size("gy")
    return (
        lax.rem(lax.axis_index("gx") + (dx + nx), nx),
        lax.rem(lax.axis_index("gy") + (dy + ny), ny),
    )


def greet_neighbours():
    for dx, dy in AROUND:
        pl.semaphore_signal(
            pltpu.get_barrier_semaphore(),
            inc=1,
            device_id=device_at(dx, dy),
            device_id_type=MESH,
        )


def meet_neighbours():
    pl.semaphore_wait(pltpu.get_barrier_semaphore(), len(AROUND))


def send(src, dst, sems, at, dx, dy):
    copy = pltpu.make_async_remote_copy(
        src_ref=src,
        dst_ref=dst,
        send_sem=sems.at[0, at],
        recv_sem=sems.at[1, at],
        device_id=device_at(dx, dy),
        device_id_type=MESH,
    )
    copy.start()
    return copy


def halo_shapes(rows, cols):
    return [
        pltpu.VMEM((2, 2, BAND, cols), F32),
        pltpu.VMEM((2, 2, rows, LANES), F32),
        pltpu.VMEM((4, 2, BAND, LANES), F32),
        pltpu.SemaphoreType.DMA((2, 8)),
    ]


def start_halo(pair, bands, sides, corners, sems):
    rows, cols = pair.shape[1:]
    low, high = pl.ds(0, BAND), pl.ds(rows - BAND, BAND)
    left, right = pl.ds(0, LANES), pl.ds(cols - LANES, LANES)
    return [
        send(pair.at[:, low, :], bands.at[0], sems, 0, -1, 0),
        send(pair.at[:, high, :], bands.at[1], sems, 1, 1, 0),
        send(pair.at[:, :, left], sides.at[0], sems, 2, 0, -1),
        send(pair.at[:, :, right], sides.at[1], sems, 3, 0, 1),
        send(pair.at[:, low, left], corners.at[0], sems, 4, -1, -1),
        send(pair.at[:, low, right], corners.at[1], sems, 5, -1, 1),
        send(pair.at[:, high, left], corners.at[2], sems, 6, 1, -1),
        send(pair.at[:, high, right], corners.at[3], sems, 7, 1, 1),
    ]


def lane_index(shape):
    return lax.broadcasted_iota(jnp.int32, shape, len(shape) - 1)


def row_index(shape):
    return lax.broadcasted_iota(jnp.int32, shape, len(shape) - 2)


def joined(which, pair, bands, sides, corners):
    def lanes(own, north, south):
        return jnp.concatenate(
            [own, jnp.where(lane_index(north.shape) < HALF, north, south)], axis=1
        )

    return jnp.concatenate(
        [
            lanes(pair[which], sides[0, which], sides[1, which]),
            lanes(bands[0, which], corners[0, which], corners[1, which]),
            lanes(bands[1, which], corners[2, which], corners[3, which]),
        ],
        axis=0,
    )


def after(field, axis):
    return pltpu.roll(field, field.shape[axis] - 1, axis)


def before(field, axis):
    return pltpu.roll(field, 1, axis)


def around_total(field):
    pair = after(field, 0) + before(field, 0)
    slanted = field + 0.5 * pair
    return pair + after(slanted, 1) + before(slanted, 1)


def inverse_of(value):
    near = pl.reciprocal(value, approx=True)
    return near * (2.0 - value * near)


def fill(k, packed, lane, side, shift):
    return jnp.where(lane == k, pltpu.roll(side, shift, 1), packed)


def by_level(levels, body, carry):
    def step(at, carry):
        for inner in range(GROUP):
            carry = body(at * GROUP + inner, carry)
        return carry

    return lax.fori_loop(0, levels // GROUP, step, carry)


def columns_kernel(
    temp_hbm,
    speed_hbm,
    mix_hbm,
    sea_hbm,
    tally_hbm,
    rain_hbm,
    temp_out,
    speed_out,
    root_out,
    ratio_out,
    scaled_out,
    temp,
    east,
    north,
    mix,
    value,
    factor,
    scale,
    sea,
    tally,
    depth,
    depth_e,
    depth_n,
    surf,
    totals,
    tail_ref,
    row_east,
    row_west,
    from_west,
    from_east,
    col_north,
    col_south,
    from_south,
    from_north,
    press_row,
    press_from_east,
    press_col,
    press_from_north,
    fix_row,
    fix_col,
    load_sems,
    chunk_sems,
    edge_sems,
    bands,
    sides,
    corners,
    halo_sems,
    total_bands,
    total_sides,
    total_corners,
    total_sems,
):
    levels, rows, cols = temp.shape
    strips = rows // BAND
    greet_neighbours()
    low, high = slice(0, LANES), slice(cols - LANES, cols)
    last_rows, last_lanes = pl.ds(rows - BAND, BAND), pl.ds(cols - LANES, LANES)
    other_rows, other_lanes = pl.ds(0, rows - BAND), pl.ds(0, cols - LANES)
    first_loads = [
        pltpu.make_async_copy(src, dst, load_sems.at[at])
        for at, (src, dst) in enumerate(
            (
                (sea_hbm, sea),
                (tally_hbm, tally),
                (rain_hbm, surf.at[1]),
                (temp_hbm, temp),
                (speed_hbm.at[1, :, :, last_lanes], north.at[:, :, last_lanes]),
                (speed_hbm.at[0, :, last_rows, :], east.at[:, last_rows, :]),
            )
        )
    ]
    for copy in first_loads:
        copy.start()
    chunks = levels // GROUP

    def load_mix(at):
        span = pl.ds(at * GROUP, GROUP)
        return pltpu.make_async_copy(mix_hbm.at[span], mix.at[span], chunk_sems.at[0, at])

    def load_speeds(at):
        span = pl.ds(at * GROUP, GROUP)
        return [
            pltpu.make_async_copy(
                speed_hbm.at[0, span, other_rows, :],
                east.at[span, other_rows, :],
                chunk_sems.at[1, at],
            ),
            pltpu.make_async_copy(
                speed_hbm.at[1, span, :, other_lanes],
                north.at[span, :, other_lanes],
                chunk_sems.at[2, at],
            ),
        ]

    for at in range(chunks):
        for copy in (load_mix(at), *load_speeds(at)):
            copy.start()
    for copy in first_loads[:3]:
        copy.wait()

    tile = (rows, cols)
    latitude = lax.axis_index("gy") * cols + lane_index(tile)
    inner = (latitude > 0) & (latitude < cols * lax.axis_size("gy") - 1)
    wet_levels = jnp.where(inner & (sea[...] == 1), tally[...], 0).astype(F32)
    depth[...] = wet_levels
    surf[0] = wet_levels
    depth_e[...] = jnp.where(
        row_index(tile) == rows - 1, 0.0, jnp.minimum(wet_levels, after(wet_levels, 0))
    )
    depth_n[...] = jnp.where(
        lane_index(tile) == cols - 1, 0.0, jnp.minimum(wet_levels, after(wet_levels, 1))
    )

    lane = lane_index((rows, LANES))
    zero_side = jnp.zeros((rows, LANES), F32)
    def pack_temp(k, carry):
        to_north, to_south = carry
        one = pl.ds(k, 1)
        row_east[0, one, :] = temp[k, rows - 1 : rows, :]
        row_west[one, :] = temp[k, 0:1, :]
        to_north = fill(k, to_north, lane, temp[k, :, high], k + 1)
        to_south = fill(k, to_south, lane, temp[k, :, low], k)
        return to_north, to_south

    def pack_speed(k, to_north):
        row_east[1, pl.ds(k, 1), :] = east[k, rows - 1 : rows, :]
        return fill(k + HALF, to_north, lane, north[k, :, high], k + 1 + HALF)

    first_loads[3].wait()
    to_north, to_south = by_level(levels, pack_temp, (zero_side, zero_side))
    col_south[...] = to_south
    meet_neighbours()
    surf_copies = start_halo(surf, bands, sides, corners, halo_sems)
    edges = [
        send(row_west, from_east, edge_sems, 0, -1, 0),
        send(col_south, from_north, edge_sems, 1, 0, -1),
    ]
    first_loads[4].wait()
    first_loads[5].wait()
    col_north[...] = by_level(levels, pack_speed, to_north)
    edges += [
        send(row_east, from_west, edge_sems, 2, 1, 0),
        send(col_north, from_south, edge_sems, 3, 0, 1),
    ]

    band = (BAND, cols)
    band_row = row_index(band)

    def upwind(open_depth, level, speed, here, there):
        flux = speed * jnp.where(speed > 0.0, here, there)
        return jnp.where(level < open_depth, flux, 0.0)

    part = [pl.ds(at * BAND, BAND) for at in range(strips)]

    def neighbour_rows(read, at, here, turned):
        if at + 1 == strips:
            return turned, None, None
        later = read(at + 1)
        later_turned = pltpu.roll(later, BAND - 1, 0)
        return jnp.where(band_row == BAND - 1, later_turned, turned), later, later_turned

    def assemble(first, carry):
        ks = [first + at for at in range(QUAD)]
        reads = [lambda at, k=k: temp[k, part[at], :] for k in ks]
        heres = [read(0) for read in reads]
        turns = [pltpu.roll(here, BAND - 1, 0) for here in heres]
        previous = [jnp.zeros(band, F32)] * QUAD
        result = []
        for at in range(strips):
            keep = carry[at]
            wet = depth[part[at], :]
            wet_e = depth_e[part[at], :]
            wet_n = depth_n[part[at], :]
            above = jnp.where(jnp.asarray(first, F32) < wet, mix[first, part[at], :], 0.0)
            for q, k in enumerate(ks):
                level = jnp.asarray(k, F32)
                here = heres[q]
                there, heres[q], next_turn = neighbour_rows(reads[q], at, here, turns[q])
                turns[q] = next_turn
                flux = upwind(wet_e, level, east[k, part[at], :], here, there)
                turned_flux = pltpu.roll(flux, 1, 0)
                total = flux - jnp.where(band_row == 0, previous[q], turned_flux)
                previous[q] = turned_flux
                flux = upwind(wet_n, level, north[k, part[at], :], here, after(here, 1))
                total = total + (flux - before(flux, 1))
                value[k, part[at], :] = here - advect_scale * total
                below = jnp.where(
                    level + 1.0 < wet, mix[jnp.minimum(k + 1, levels - 1), part[at], :], 0.0
                )
                inverse_pivot = inverse_of((1.0 + below) + above * keep)
                scale[k, part[at], :] = inverse_pivot
                leading = below * inverse_pivot
                factor[k, part[at], :] = leading
                keep = 1.0 - leading
                above = below
            result.append(keep)
        return tuple(result)

    def assemble_chunk(at, carry):
        @pl.when(at + 1 < chunks)
        def _():
            load_mix(at + 1).wait()

        for copy in load_speeds(at):
            copy.wait()

        def step(half, carry):
            return assemble(at * GROUP + QUAD * half, carry)

        return lax.fori_loop(0, GROUP // QUAD, step, carry)

    load_mix(0).wait()
    lax.fori_loop(0, chunks, assemble_chunk, (jnp.zeros(band, F32),) * strips)

    for copy in surf_copies:
        copy.wait()
    wide = joined(0, surf, bands, sides, corners)
    last_e = jnp.minimum(wide[rows - 1 : rows, :cols], wide[rows : rows + 1, :cols])
    last_n = jnp.minimum(wide[:rows, cols - 1 : cols], wide[:rows, cols : cols + 1])
    open_w = jnp.minimum(wide[0:1, :cols], wide[-1:, :cols])
    open_s = jnp.minimum(wide[:rows, 0:1], wide[:rows, -1:])

    for copy in edges:
        copy.wait()
    level_row = row_index((levels, cols)).astype(F32)
    level_lane = lane.astype(F32)
    flux_w = upwind(open_w, level_row, from_west[1], from_west[0], row_west[...])
    flux_e = upwind(last_e, level_row, row_east[1], row_east[0], from_east[...])
    flux_s = upwind(
        open_s, level_lane, pltpu.roll(from_south[...], HALF, 1), from_south[...], col_south[...]
    )
    flux_n = upwind(
        last_n, level_lane, pltpu.roll(col_north[...], HALF, 1), col_north[...], from_north[...]
    )
    from_west[0] = advect_scale * flux_w
    from_west[1] = advect_scale * flux_e
    from_south[...] = advect_scale * flux_s
    from_north[...] = advect_scale * flux_n

    middle = [jnp.zeros((rows, cols - 2 * LANES), F32)] if cols > 2 * LANES else []

    def forward(k, x):
        one = pl.ds(k, 1)
        rim = jnp.concatenate(
            [
                jnp.where(lane == 0, pltpu.roll(from_south[...], LANES - k, 1), 0.0),
                *middle,
                jnp.where(
                    lane == LANES - 1, -pltpu.roll(from_north[...], LANES - 1 - k, 1), 0.0
                ),
            ],
            axis=1,
        )
        source = value[k] + rim
        source = jnp.concatenate(
            [
                source[:BAND] + jnp.where(band_row == 0, from_west[0, one, :], 0.0),
                source[BAND : rows - BAND],
                source[rows - BAND :]
                - jnp.where(band_row == BAND - 1, from_west[1, one, :], 0.0),
            ],
            axis=0,
        )
        above = jnp.where(jnp.asarray(k, F32) < depth[...], mix[k], 0.0)
        x = (source + above * x) * scale[k]
        temp[k] = x
        return x

    by_level(levels, forward, jnp.zeros(tile, F32))

    slope = force_scale / levels

    def backward(step, carry):
        x, tail, to_north, to_south = carry
        k = levels - 1 - step
        one = pl.ds(k, 1)
        x = temp[k] + factor[k] * x
        temp_out[k] = x
        share = slope * x
        tail = tail + share
        press = tail - 0.5 * share
        value[k] = press
        press_row[0, one, :] = press[0:1, :]
        press_row[1, one, :] = press[rows - 1 : rows, :]
        to_north = fill(k, to_north, lane, press[:, high], k + 1)
        to_south = fill(k, to_south, lane, press[:, low], k)
        return x, tail, to_north, to_south

    zero_tile = jnp.zeros(tile, F32)
    x, tail, to_north, to_south = by_level(
        levels, backward, (zero_tile, zero_tile, zero_side, zero_side)
    )
    tail_ref[...] = tail
    press_row[0] -= tail[0:1, :]
    press_row[1] -= tail[rows - 1 : rows, :]
    press_col[0] = to_south - tail[:, 0:1]
    press_col[1] = to_north - tail[:, cols - 1 : cols]
    press = [
        send(press_row.at[0], press_from_east, edge_sems, 4, -1, 0),
        send(press_col.at[0], press_from_north, edge_sems, 5, 0, -1),
    ]

    totals[...] = jnp.zeros(totals.shape, F32)

    def momentum(step, carry):
        ks = [step * QUAD + at for at in range(QUAD)]
        reads = [lambda at, k=k: value[k, part[at], :] - tail_ref[part[at], :] for k in ks]
        heres = [read(0) for read in reads]
        turns = [pltpu.roll(here, BAND - 1, 0) for here in heres]
        for at in range(strips):
            wet_e = depth_e[part[at], :]
            wet_n = depth_n[part[at], :]
            sums = [totals[0, part[at], :], totals[1, part[at], :]]
            for q, k in enumerate(ks):
                level = jnp.asarray(k, F32)
                here = heres[q]
                there, heres[q], next_turn = neighbour_rows(reads[q], at, here, turns[q])
                turns[q] = next_turn
                speed = east[k, part[at], :] + (here - there)
                speed = jnp.where(level < wet_e, speed, 0.0)
                speed_out[0, k, part[at], :] = speed
                sums[0] = sums[0] + speed
                speed = north[k, part[at], :] + (here - after(here, 1))
                speed = jnp.where(level < wet_n, speed, 0.0)
                speed_out[1, k, part[at], :] = speed
                sums[1] = sums[1] + speed
            totals[0, part[at], :] = sums[0]
            totals[1, part[at], :] = sums[1]
        return carry

    lax.fori_loop(0, levels // QUAD, momentum, 0)

    for copy in press:
        copy.wait()
    speed_e = row_east[1] + (press_row[1] - press_from_east[...])
    speed_e = jnp.where(level_row < last_e, speed_e, 0.0)
    speed_n = pltpu.roll(col_north[...], HALF, 1) + (press_col[1] - press_from_north[...])
    speed_n = jnp.where(level_lane < last_n, speed_n, 0.0)
    fix_row[...] = speed_e
    fix_col[...] = speed_n
    totals[0, rows - 1 : rows, :] = jnp.sum(speed_e, axis=0, keepdims=True)
    totals[1, :, high] += jnp.where(
        lane == LANES - 1, jnp.sum(speed_n, axis=1, keepdims=True), 0.0
    )
    total_copies = start_halo(totals, total_bands, total_sides, total_corners, total_sems)

    def add_last(k, carry):
        speed_out[0, k, rows - 1 : rows, :] = fix_row[pl.ds(k, 1), :]
        speed_out[1, k, :, high] += jnp.where(
            lane == LANES - 1, pltpu.roll(fix_col[...], LANES - 1 - k, 1), 0.0
        )
        return carry

    by_level(levels, add_last, 0)

    source = source_scale * joined(1, surf, bands, sides, corners)
    root = jnp.sqrt(wide / levels)
    inverse = 1.0 / (damping + root * around_total(root))
    root_out[...] = root
    ratio_out[...] = root * inverse

    for copy in total_copies:
        copy.wait()
    total_e = joined(0, totals, total_bands, total_sides, total_corners)
    total_n = joined(1, totals, total_bands, total_sides, total_corners)
    divergence = total_e - before(total_e, 0) + total_n - before(total_n, 1)
    forcing = source - (divergence_scale / levels) * divergence
    scaled_out[...] = jnp.where(root > 0.0, forcing * inverse, 0.0)


def surface_kernel(
    temp_in, speed_in, root_in, ratio_in, scaled_in, temp_out, speed_out, out, sems
):
    rows, cols = out.shape
    copies = [
        pltpu.make_async_copy(temp_in, temp_out, sems.at[0]),
        pltpu.make_async_copy(speed_in.at[0], speed_out.at[0], sems.at[1]),
        pltpu.make_async_copy(speed_in.at[1], speed_out.at[1], sems.at[2]),
    ]
    for copy in copies:
        copy.start()
    root = root_in[...]
    ratio = ratio_in[...]
    scaled = scaled_in[...]
    update = scaled * (1.0 / cheb_gamma)
    iterate = update
    omega = 2.0 / cheb_gamma
    for _ in range(1, ITERS):
        omega = 1.0 / (cheb_gamma - omega / (4.0 * cheb_alpha * cheb_alpha))
        residual = scaled - iterate + ratio * around_total(root * iterate)
        update = omega * residual + (cheb_gamma * omega - 1.0) * update
        iterate = iterate + update
    out[...] = iterate[:rows, :cols]
    for copy in copies:
        copy.wait()


def local(temp, speeds, mix, sea, tally, rain):
    levels, rows, cols = temp.shape
    wide = pltpu.VMEM((rows + 2 * BAND, cols + LANES), F32)
    vmem = pl.BlockSpec(memory_space=pltpu.VMEM)
    field = pltpu.VMEM((levels, rows, cols), F32)
    plane = pltpu.VMEM((rows, cols), F32)
    plane_int = pltpu.VMEM((rows, cols), jnp.int32)
    two_planes = pltpu.VMEM((2, rows, cols), F32)
    row_set = pltpu.VMEM((levels, cols), F32)
    row_sets = pltpu.VMEM((2, levels, cols), F32)
    col_set = pltpu.VMEM((rows, LANES), F32)
    col_sets = pltpu.VMEM((2, rows, LANES), F32)
    inputs = [
        pltpu.with_memory_space_constraint(array, pltpu.HBM)
        for array in (temp, speeds, mix, sea, tally, rain)
    ]
    temp_next, speed_next, root, ratio, scaled = pl.pallas_call(
        columns_kernel,
        out_shape=[field, pltpu.VMEM((2, levels, rows, cols), F32), wide, wide, wide],
        in_specs=[pl.BlockSpec(memory_space=pltpu.HBM)] * 6,
        out_specs=[vmem] * 5,
        scratch_shapes=[field] * 7
        + [plane_int] * 2
        + [plane] * 3
        + [two_planes, two_planes, plane]
        + [row_sets, row_set, row_sets, row_set]
        + [col_set] * 4
        + [row_sets, row_set, col_sets, col_set]
        + [row_set, col_set]
        + [
            pltpu.SemaphoreType.DMA((6,)),
            pltpu.SemaphoreType.DMA((3, levels // GROUP)),
            pltpu.SemaphoreType.DMA((2, 6)),
        ]
        + halo_shapes(rows, cols) * 2,
        compiler_params=pltpu.CompilerParams(
            collective_id=0, has_side_effects=True, vmem_limit_bytes=48 * 2**20
        ),
        name="columns",
    )(*inputs)
    held = [
        pltpu.with_memory_space_constraint(array, pltpu.VMEM)
        for array in (temp_next, speed_next, root, ratio, scaled)
    ]
    return pl.pallas_call(
        surface_kernel,
        out_shape=[
            jax.ShapeDtypeStruct(temp.shape, F32),
            jax.ShapeDtypeStruct(speeds.shape, F32),
            jax.ShapeDtypeStruct((rows, cols), F32),
        ],
        in_specs=[vmem] * 5,
        out_specs=[pl.BlockSpec(memory_space=pltpu.HBM)] * 2 + [vmem],
        scratch_shapes=[pltpu.SemaphoreType.DMA((3,))],
        compiler_params=pltpu.CompilerParams(vmem_limit_bytes=32 * 2**20),
        name="surface",
    )(*held)


def solution(mesh):
    tile = P("gx", "gy")
    column = P(None, "gx", "gy")
    pair = P(None, None, "gx", "gy")
    return jax.shard_map(
        local,
        mesh=mesh,
        in_specs=(column, pair, column, tile, tile, tile),
        out_specs=(column, pair, tile),
        check_vma=False,
    )
```

```python
import jax
import jax.numpy as jnp
from jax import lax
from jax.experimental import pallas as pl
from jax.experimental.pallas import tpu as pltpu
from jax.sharding import PartitionSpec as P

ITERS = 6
damping = 0.05
lower_bound = 0.02
upper_bound = 2.0
cheb_alpha = 2.0 / (upper_bound - lower_bound)
cheb_gamma = (upper_bound + lower_bound) / 2.0
advect_scale = 0.4
force_scale = 4.0
source_scale = 0.5
divergence_scale = 4.0

MESH = pl.DeviceIdType.MESH
LANES = 128
HALF = LANES // 2
GROUP = 8
QUAD = 4
BAND = 8
F32 = jnp.float32
AROUND = ((1, 0), (-1, 0), (0, 1), (0, -1), (1, 1), (1, -1), (-1, 1), (-1, -1))


def device_at(dx, dy):
    nx, ny = lax.axis_size("gx"), lax.axis_size("gy")
    return (
        lax.rem(lax.axis_index("gx") + (dx + nx), nx),
        lax.rem(lax.axis_index("gy") + (dy + ny), ny),
    )


def greet_neighbours():
    for dx, dy in AROUND:
        pl.semaphore_signal(
            pltpu.get_barrier_semaphore(),
            inc=1,
            device_id=device_at(dx, dy),
            device_id_type=MESH,
        )


def meet_neighbours():
    pl.semaphore_wait(pltpu.get_barrier_semaphore(), len(AROUND))


def send(src, dst, sems, at, dx, dy):
    copy = pltpu.make_async_remote_copy(
        src_ref=src,
        dst_ref=dst,
        send_sem=sems.at[0, at],
        recv_sem=sems.at[1, at],
        device_id=device_at(dx, dy),
        device_id_type=MESH,
    )
    copy.start()
    return copy


def halo_shapes(rows, cols):
    return [
        pltpu.VMEM((2, 2, BAND, cols), F32),
        pltpu.VMEM((2, 2, rows, LANES), F32),
        pltpu.VMEM((4, 2, BAND, LANES), F32),
        pltpu.SemaphoreType.DMA((2, 8)),
    ]


def start_halo(pair, bands, sides, corners, sems):
    rows, cols = pair.shape[1:]
    low, high = pl.ds(0, BAND), pl.ds(rows - BAND, BAND)
    left, right = pl.ds(0, LANES), pl.ds(cols - LANES, LANES)
    return [
        send(pair.at[:, low, :], bands.at[0], sems, 0, -1, 0),
        send(pair.at[:, high, :], bands.at[1], sems, 1, 1, 0),
        send(pair.at[:, :, left], sides.at[0], sems, 2, 0, -1),
        send(pair.at[:, :, right], sides.at[1], sems, 3, 0, 1),
        send(pair.at[:, low, left], corners.at[0], sems, 4, -1, -1),
        send(pair.at[:, low, right], corners.at[1], sems, 5, -1, 1),
        send(pair.at[:, high, left], corners.at[2], sems, 6, 1, -1),
        send(pair.at[:, high, right], corners.at[3], sems, 7, 1, 1),
    ]


def lane_index(shape):
    return lax.broadcasted_iota(jnp.int32, shape, len(shape) - 1)


def row_index(shape):
    return lax.broadcasted_iota(jnp.int32, shape, len(shape) - 2)


def joined(which, pair, bands, sides, corners):
    def lanes(own, north, south):
        return jnp.concatenate(
            [own, jnp.where(lane_index(north.shape) < HALF, north, south)], axis=1
        )

    return jnp.concatenate(
        [
            lanes(pair[which], sides[0, which], sides[1, which]),
            lanes(bands[0, which], corners[0, which], corners[1, which]),
            lanes(bands[1, which], corners[2, which], corners[3, which]),
        ],
        axis=0,
    )


def after(field, axis):
    return pltpu.roll(field, field.shape[axis] - 1, axis)


def before(field, axis):
    return pltpu.roll(field, 1, axis)


def around_total(field):
    pair = after(field, 0) + before(field, 0)
    slanted = field + 0.5 * pair
    return pair + after(slanted, 1) + before(slanted, 1)


def inverse_of(value):
    near = pl.reciprocal(value, approx=True)
    return near * (2.0 - value * near)


def fill(k, packed, lane, side, shift):
    return jnp.where(lane == k, pltpu.roll(side, shift, 1), packed)


def by_level(levels, body, carry):
    def step(at, carry):
        for inner in range(GROUP):
            carry = body(at * GROUP + inner, carry)
        return carry

    return lax.fori_loop(0, levels // GROUP, step, carry)


def columns_kernel(
    temp_hbm,
    speed_hbm,
    mix_hbm,
    sea_hbm,
    tally_hbm,
    rain_hbm,
    temp_out,
    speed_out,
    root_out,
    ratio_out,
    scaled_out,
    temp,
    east,
    north,
    mix,
    value,
    factor,
    scale,
    sea,
    tally,
    depth,
    depth_e,
    depth_n,
    surf,
    totals,
    tail_ref,
    row_east,
    row_west,
    from_west,
    from_east,
    col_north,
    col_south,
    from_south,
    from_north,
    press_row,
    press_from_east,
    press_col,
    press_from_north,
    last_row_low,
    last_row_rest,
    last_col,
    fix_row,
    fix_col,
    load_sems,
    chunk_sems,
    edge_sems,
    bands,
    sides,
    corners,
    halo_sems,
    total_bands,
    total_sides,
    total_corners,
    total_sems,
):
    levels, rows, cols = temp.shape
    strips = rows // BAND
    greet_neighbours()
    low, high = slice(0, LANES), slice(cols - LANES, cols)
    last_rows, last_lanes = pl.ds(rows - BAND, BAND), pl.ds(cols - LANES, LANES)
    other_rows, other_lanes = pl.ds(0, rows - BAND), pl.ds(0, cols - LANES)
    first_loads = [
        pltpu.make_async_copy(src, dst, load_sems.at[at])
        for at, (src, dst) in enumerate(
            (
                (sea_hbm, sea),
                (tally_hbm, tally),
                (rain_hbm, surf.at[1]),
                (temp_hbm, temp),
                (speed_hbm.at[1, :, :, last_lanes], north.at[:, :, last_lanes]),
                (speed_hbm.at[0, :, last_rows, :], east.at[:, last_rows, :]),
            )
        )
    ]
    for copy in first_loads:
        copy.start()
    chunks = levels // GROUP

    def load_mix(at):
        span = pl.ds(at * GROUP, GROUP)
        return pltpu.make_async_copy(mix_hbm.at[span], mix.at[span], chunk_sems.at[0, at])

    def load_speeds(at):
        span = pl.ds(at * GROUP, GROUP)
        return [
            pltpu.make_async_copy(
                speed_hbm.at[0, span, other_rows, :],
                east.at[span, other_rows, :],
                chunk_sems.at[1, at],
            ),
            pltpu.make_async_copy(
                speed_hbm.at[1, span, :, other_lanes],
                north.at[span, :, other_lanes],
                chunk_sems.at[2, at],
            ),
        ]

    for at in range(chunks):
        for copy in (load_mix(at), *load_speeds(at)):
            copy.start()
    for copy in first_loads[:3]:
        copy.wait()

    tile = (rows, cols)
    latitude = lax.axis_index("gy") * cols + lane_index(tile)
    inner = (latitude > 0) & (latitude < cols * lax.axis_size("gy") - 1)
    wet_levels = jnp.where(inner & (sea[...] == 1), tally[...], 0).astype(F32)
    depth[...] = wet_levels
    surf[0] = wet_levels
    depth_e[...] = jnp.where(
        row_index(tile) == rows - 1, 0.0, jnp.minimum(wet_levels, after(wet_levels, 0))
    )
    depth_n[...] = jnp.where(
        lane_index(tile) == cols - 1, 0.0, jnp.minimum(wet_levels, after(wet_levels, 1))
    )

    lane = lane_index((rows, LANES))
    zero_side = jnp.zeros((rows, LANES), F32)
    def pack_temp(k, carry):
        to_north, to_south = carry
        one = pl.ds(k, 1)
        row_east[0, one, :] = temp[k, rows - 1 : rows, :]
        row_west[one, :] = temp[k, 0:1, :]
        to_north = fill(k, to_north, lane, temp[k, :, high], k + 1)
        to_south = fill(k, to_south, lane, temp[k, :, low], k)
        return to_north, to_south

    def pack_speed(k, to_north):
        row_east[1, pl.ds(k, 1), :] = east[k, rows - 1 : rows, :]
        return fill(k + HALF, to_north, lane, north[k, :, high], k + 1 + HALF)

    first_loads[3].wait()
    to_north, to_south = by_level(levels, pack_temp, (zero_side, zero_side))
    col_south[...] = to_south
    meet_neighbours()
    surf_copies = start_halo(surf, bands, sides, corners, halo_sems)
    edges = [
        send(row_west, from_east, edge_sems, 0, -1, 0),
        send(col_south, from_north, edge_sems, 1, 0, -1),
    ]
    first_loads[4].wait()
    first_loads[5].wait()
    col_north[...] = by_level(levels, pack_speed, to_north)
    edges += [
        send(row_east, from_west, edge_sems, 2, 1, 0),
        send(col_north, from_south, edge_sems, 3, 0, 1),
    ]

    band = (BAND, cols)
    band_row = row_index(band)

    def upwind(open_depth, level, speed, here, there):
        flux = speed * jnp.where(speed > 0.0, here, there)
        return jnp.where(level < open_depth, flux, 0.0)

    part = [pl.ds(at * BAND, BAND) for at in range(strips)]

    def neighbour_rows(read, at, here, turned):
        if at + 1 == strips:
            return turned, None, None
        later = read(at + 1)
        later_turned = pltpu.roll(later, BAND - 1, 0)
        return jnp.where(band_row == BAND - 1, later_turned, turned), later, later_turned

    def assemble(first, carry):
        ks = [first + at for at in range(QUAD)]
        reads = [lambda at, k=k: temp[k, part[at], :] for k in ks]
        heres = [read(0) for read in reads]
        turns = [pltpu.roll(here, BAND - 1, 0) for here in heres]
        previous = [jnp.zeros(band, F32)] * QUAD
        result = []
        for at in range(strips):
            keep = carry[at]
            wet = depth[part[at], :]
            wet_e = depth_e[part[at], :]
            wet_n = depth_n[part[at], :]
            above = jnp.where(jnp.asarray(first, F32) < wet, mix[first, part[at], :], 0.0)
            for q, k in enumerate(ks):
                level = jnp.asarray(k, F32)
                here = heres[q]
                there, heres[q], next_turn = neighbour_rows(reads[q], at, here, turns[q])
                turns[q] = next_turn
                flux = upwind(wet_e, level, east[k, part[at], :], here, there)
                turned_flux = pltpu.roll(flux, 1, 0)
                total = flux - jnp.where(band_row == 0, previous[q], turned_flux)
                previous[q] = turned_flux
                flux = upwind(wet_n, level, north[k, part[at], :], here, after(here, 1))
                total = total + (flux - before(flux, 1))
                value[k, part[at], :] = here - advect_scale * total
                below = jnp.where(
                    level + 1.0 < wet, mix[jnp.minimum(k + 1, levels - 1), part[at], :], 0.0
                )
                inverse_pivot = inverse_of((1.0 + below) + above * keep)
                scale[k, part[at], :] = inverse_pivot
                leading = below * inverse_pivot
                factor[k, part[at], :] = leading
                keep = 1.0 - leading
                above = below
            result.append(keep)
        return tuple(result)

    def assemble_chunk(at, carry):
        @pl.when(at + 1 < chunks)
        def _():
            load_mix(at + 1).wait()

        for copy in load_speeds(at):
            copy.wait()

        def step(half, carry):
            return assemble(at * GROUP + QUAD * half, carry)

        return lax.fori_loop(0, GROUP // QUAD, step, carry)

    load_mix(0).wait()
    lax.fori_loop(0, chunks, assemble_chunk, (jnp.zeros(band, F32),) * strips)

    for copy in surf_copies:
        copy.wait()
    wide = joined(0, surf, bands, sides, corners)
    last_e = jnp.minimum(wide[rows - 1 : rows, :cols], wide[rows : rows + 1, :cols])
    last_n = jnp.minimum(wide[:rows, cols - 1 : cols], wide[:rows, cols : cols + 1])
    open_w = jnp.minimum(wide[0:1, :cols], wide[-1:, :cols])
    open_s = jnp.minimum(wide[:rows, 0:1], wide[:rows, -1:])

    for copy in edges:
        copy.wait()
    level_row = row_index((levels, cols)).astype(F32)
    level_lane = lane.astype(F32)
    flux_w = upwind(open_w, level_row, from_west[1], from_west[0], row_west[...])
    flux_e = upwind(last_e, level_row, row_east[1], row_east[0], from_east[...])
    flux_s = upwind(
        open_s, level_lane, pltpu.roll(from_south[...], HALF, 1), from_south[...], col_south[...]
    )
    flux_n = upwind(
        last_n, level_lane, pltpu.roll(col_north[...], HALF, 1), col_north[...], from_north[...]
    )
    from_west[0] = advect_scale * flux_w
    from_west[1] = advect_scale * flux_e
    from_south[...] = advect_scale * flux_s
    from_north[...] = advect_scale * flux_n

    rest = cols - LANES
    whole_low = (rows, 0, LANES)
    band_rest = (BAND, LANES, cols)
    whole_rest = (rows, LANES, cols)

    def forward(k, x, region):
        size, start, stop = region
        one = pl.ds(k, 1)
        source = value[k, :size, start:stop]
        if start == 0:
            rim = jnp.where(lane == 0, pltpu.roll(from_south[...], LANES - k, 1), 0.0)
        else:
            turned = pltpu.roll(from_north[:size, :], LANES - 1 - k, 1)
            rim = jnp.where(lane[:size] == LANES - 1, -turned, 0.0)
            if rest > LANES:
                rim = jnp.concatenate([jnp.zeros((size, rest - LANES), F32), rim], axis=1)
        source = source + rim
        row = band_row[:, : stop - start]
        pieces = [source[:BAND] + jnp.where(row == 0, from_west[0, one, :][:, start:stop], 0.0)]
        if size == rows:
            pieces += [
                source[BAND : rows - BAND],
                source[rows - BAND :]
                - jnp.where(row == BAND - 1, from_west[1, one, :][:, start:stop], 0.0),
            ]
        source = jnp.concatenate(pieces, axis=0) if len(pieces) > 1 else pieces[0]
        above = jnp.where(
            jnp.asarray(k, F32) < depth[:size, start:stop], mix[k, :size, start:stop], 0.0
        )
        x = (source + above * x) * scale[k, :size, start:stop]
        temp[k, :size, start:stop] = x
        return x

    slope = force_scale / levels

    def backward(k, x, tail, region):
        size, start, stop = region
        x = temp[k, :size, start:stop] + factor[k, :size, start:stop] * x
        share = slope * x
        tail = tail + share
        press = tail - 0.5 * share
        if size == rows:
            temp_out[k, :, start:stop] = x
            value[k, :, start:stop] = press
            last = last_row_low if start == 0 else last_row_rest
            last[pl.ds(k, 1), :] = press[rows - 1 :, :]
        return x, tail, press

    zero_low = jnp.zeros((rows, LANES), F32)
    zero_band = jnp.zeros((BAND, rest), F32)
    zero_rest = jnp.zeros((rows, rest), F32)

    def forward_first(k, carry):
        return forward(k, carry[0], whole_low), forward(k, carry[1], band_rest)

    def backward_first(step, carry):
        x, tail, x_band, tail_band, packed = carry
        k = levels - 1 - step
        one = pl.ds(k, 1)
        x, tail, press = backward(k, x, tail, whole_low)
        packed = fill(k, packed, lane, press, k)
        x_band, tail_band, press_band = backward(k, x_band, tail_band, band_rest)
        press_row[one, :] = jnp.concatenate([press[0:1, :], press_band[0:1, :]], axis=1)
        return x, tail, x_band, tail_band, packed

    def backward_rest(step, carry):
        x, tail, packed = carry
        k = levels - 1 - step
        x, tail, press = backward(k, x, tail, whole_rest)
        packed = fill(k, packed, lane, press[:, rest - LANES :], k + 1)
        return x, tail, packed

    by_level(levels, forward_first, (zero_low, zero_band))
    x, tail, x_band, tail_band, packed = by_level(
        levels, backward_first, (zero_low, zero_low, zero_band, zero_band, zero_side)
    )
    tail_ref[:, :LANES] = tail
    press_row[:, :LANES] -= tail[0:1, :]
    press_row[:, LANES:] -= tail_band[0:1, :]
    last_row_low[...] -= tail[rows - 1 :, :]
    press_col[...] = packed - tail[:, 0:1]
    press = [
        send(press_row, press_from_east, edge_sems, 4, -1, 0),
        send(press_col, press_from_north, edge_sems, 5, 0, -1),
    ]
    by_level(levels, lambda k, x: forward(k, x, whole_rest), zero_rest)
    x, tail, packed = by_level(levels, backward_rest, (zero_rest, zero_rest, zero_side))
    tail_ref[:, LANES:] = tail
    last_row_rest[...] -= tail[rows - 1 :, :]
    last_col[...] = packed - tail[:, rest - 1 :]

    totals[...] = jnp.zeros(totals.shape, F32)

    def momentum(step, carry):
        ks = [step * QUAD + at for at in range(QUAD)]
        reads = [lambda at, k=k: value[k, part[at], :] - tail_ref[part[at], :] for k in ks]
        heres = [read(0) for read in reads]
        turns = [pltpu.roll(here, BAND - 1, 0) for here in heres]
        for at in range(strips):
            wet_e = depth_e[part[at], :]
            wet_n = depth_n[part[at], :]
            sums = [totals[0, part[at], :], totals[1, part[at], :]]
            for q, k in enumerate(ks):
                level = jnp.asarray(k, F32)
                here = heres[q]
                there, heres[q], next_turn = neighbour_rows(reads[q], at, here, turns[q])
                turns[q] = next_turn
                speed = east[k, part[at], :] + (here - there)
                speed = jnp.where(level < wet_e, speed, 0.0)
                speed_out[0, k, part[at], :] = speed
                sums[0] = sums[0] + speed
                speed = north[k, part[at], :] + (here - after(here, 1))
                speed = jnp.where(level < wet_n, speed, 0.0)
                speed_out[1, k, part[at], :] = speed
                sums[1] = sums[1] + speed
            totals[0, part[at], :] = sums[0]
            totals[1, part[at], :] = sums[1]
        return carry

    lax.fori_loop(0, levels // QUAD, momentum, 0)

    for copy in press:
        copy.wait()
    last_row = jnp.concatenate([last_row_low[...], last_row_rest[...]], axis=1)
    speed_e = row_east[1] + (last_row - press_from_east[...])
    speed_e = jnp.where(level_row < last_e, speed_e, 0.0)
    speed_n = pltpu.roll(col_north[...], HALF, 1) + (last_col[...] - press_from_north[...])
    speed_n = jnp.where(level_lane < last_n, speed_n, 0.0)
    fix_row[...] = speed_e
    fix_col[...] = speed_n
    totals[0, rows - 1 : rows, :] = jnp.sum(speed_e, axis=0, keepdims=True)
    totals[1, :, high] += jnp.where(
        lane == LANES - 1, jnp.sum(speed_n, axis=1, keepdims=True), 0.0
    )
    total_copies = start_halo(totals, total_bands, total_sides, total_corners, total_sems)

    def add_last(k, carry):
        speed_out[0, k, rows - 1 : rows, :] = fix_row[pl.ds(k, 1), :]
        speed_out[1, k, :, high] += jnp.where(
            lane == LANES - 1, pltpu.roll(fix_col[...], LANES - 1 - k, 1), 0.0
        )
        return carry

    by_level(levels, add_last, 0)

    source = source_scale * joined(1, surf, bands, sides, corners)
    root = jnp.sqrt(wide / levels)
    inverse = 1.0 / (damping + root * around_total(root))
    root_out[...] = root
    ratio_out[...] = root * inverse

    for copy in total_copies:
        copy.wait()
    total_e = joined(0, totals, total_bands, total_sides, total_corners)
    total_n = joined(1, totals, total_bands, total_sides, total_corners)
    divergence = total_e - before(total_e, 0) + total_n - before(total_n, 1)
    forcing = source - (divergence_scale / levels) * divergence
    scaled_out[...] = jnp.where(root > 0.0, forcing * inverse, 0.0)


def surface_kernel(
    temp_in, speed_in, root_in, ratio_in, scaled_in, temp_out, speed_out, out, sems
):
    rows, cols = out.shape
    copies = [
        pltpu.make_async_copy(temp_in, temp_out, sems.at[0]),
        pltpu.make_async_copy(speed_in.at[0], speed_out.at[0], sems.at[1]),
        pltpu.make_async_copy(speed_in.at[1], speed_out.at[1], sems.at[2]),
    ]
    for copy in copies:
        copy.start()
    root = root_in[...]
    ratio = ratio_in[...]
    scaled = scaled_in[...]
    update = scaled * (1.0 / cheb_gamma)
    iterate = update
    omega = 2.0 / cheb_gamma
    for _ in range(1, ITERS):
        omega = 1.0 / (cheb_gamma - omega / (4.0 * cheb_alpha * cheb_alpha))
        residual = scaled - iterate + ratio * around_total(root * iterate)
        update = omega * residual + (cheb_gamma * omega - 1.0) * update
        iterate = iterate + update
    out[...] = iterate[:rows, :cols]
    for copy in copies:
        copy.wait()


def local(temp, speeds, mix, sea, tally, rain):
    levels, rows, cols = temp.shape
    wide = pltpu.VMEM((rows + 2 * BAND, cols + LANES), F32)
    vmem = pl.BlockSpec(memory_space=pltpu.VMEM)
    field = pltpu.VMEM((levels, rows, cols), F32)
    plane = pltpu.VMEM((rows, cols), F32)
    plane_int = pltpu.VMEM((rows, cols), jnp.int32)
    two_planes = pltpu.VMEM((2, rows, cols), F32)
    row_set = pltpu.VMEM((levels, cols), F32)
    row_sets = pltpu.VMEM((2, levels, cols), F32)
    col_set = pltpu.VMEM((rows, LANES), F32)
    inputs = [
        pltpu.with_memory_space_constraint(array, pltpu.HBM)
        for array in (temp, speeds, mix, sea, tally, rain)
    ]
    temp_next, speed_next, root, ratio, scaled = pl.pallas_call(
        columns_kernel,
        out_shape=[field, pltpu.VMEM((2, levels, rows, cols), F32), wide, wide, wide],
        in_specs=[pl.BlockSpec(memory_space=pltpu.HBM)] * 6,
        out_specs=[vmem] * 5,
        scratch_shapes=[field] * 7
        + [plane_int] * 2
        + [plane] * 3
        + [two_planes, two_planes, plane]
        + [row_sets, row_set, row_sets, row_set]
        + [col_set] * 4
        + [row_set, row_set, col_set, col_set]
        + [pltpu.VMEM((levels, LANES), F32), pltpu.VMEM((levels, cols - LANES), F32), col_set]
        + [row_set, col_set]
        + [
            pltpu.SemaphoreType.DMA((6,)),
            pltpu.SemaphoreType.DMA((3, levels // GROUP)),
            pltpu.SemaphoreType.DMA((2, 6)),
        ]
        + halo_shapes(rows, cols) * 2,
        compiler_params=pltpu.CompilerParams(
            collective_id=0, has_side_effects=True, vmem_limit_bytes=48 * 2**20
        ),
        name="columns",
    )(*inputs)
    held = [
        pltpu.with_memory_space_constraint(array, pltpu.VMEM)
        for array in (temp_next, speed_next, root, ratio, scaled)
    ]
    return pl.pallas_call(
        surface_kernel,
        out_shape=[
            jax.ShapeDtypeStruct(temp.shape, F32),
            jax.ShapeDtypeStruct(speeds.shape, F32),
            jax.ShapeDtypeStruct((rows, cols), F32),
        ],
        in_specs=[vmem] * 5,
        out_specs=[pl.BlockSpec(memory_space=pltpu.HBM)] * 2 + [vmem],
        scratch_shapes=[pltpu.SemaphoreType.DMA((3,))],
        compiler_params=pltpu.CompilerParams(vmem_limit_bytes=32 * 2**20),
        name="surface",
    )(*held)


def solution(mesh):
    tile = P("gx", "gy")
    column = P(None, "gx", "gy")
    pair = P(None, None, "gx", "gy")
    return jax.shard_map(
        local,
        mesh=mesh,
        in_specs=(column, pair, column, tile, tile, tile),
        out_specs=(column, pair, tile),
        check_vma=False,
    )
```

```python
import jax
import jax.numpy as jnp
from jax import lax
from jax.experimental import pallas as pl
from jax.experimental.pallas import tpu as pltpu
from jax.sharding import PartitionSpec as P

ITERS = 6
damping = 0.05
lower_bound = 0.02
upper_bound = 2.0
cheb_alpha = 2.0 / (upper_bound - lower_bound)
cheb_gamma = (upper_bound + lower_bound) / 2.0
advect_scale = 0.4
force_scale = 4.0
source_scale = 0.5
divergence_scale = 4.0

MESH = pl.DeviceIdType.MESH
LANES = 128
HALF = LANES // 2
GROUP = 8
QUAD = 4
BAND = 8
F32 = jnp.float32
AROUND = ((1, 0), (-1, 0), (0, 1), (0, -1), (1, 1), (1, -1), (-1, 1), (-1, -1))


def device_at(dx, dy):
    nx, ny = lax.axis_size("gx"), lax.axis_size("gy")
    return (
        lax.rem(lax.axis_index("gx") + (dx + nx), nx),
        lax.rem(lax.axis_index("gy") + (dy + ny), ny),
    )


def greet_neighbours():
    for dx, dy in AROUND:
        pl.semaphore_signal(
            pltpu.get_barrier_semaphore(),
            inc=1,
            device_id=device_at(dx, dy),
            device_id_type=MESH,
        )


def meet_neighbours():
    pl.semaphore_wait(pltpu.get_barrier_semaphore(), len(AROUND))


def send(src, dst, sems, at, dx, dy):
    copy = pltpu.make_async_remote_copy(
        src_ref=src,
        dst_ref=dst,
        send_sem=sems.at[0, at],
        recv_sem=sems.at[1, at],
        device_id=device_at(dx, dy),
        device_id_type=MESH,
    )
    copy.start()
    return copy


def halo_shapes(rows, cols):
    return [
        pltpu.VMEM((2, 2, BAND, cols), F32),
        pltpu.VMEM((2, 2, rows, LANES), F32),
        pltpu.VMEM((4, 2, BAND, LANES), F32),
        pltpu.SemaphoreType.DMA((2, 8)),
    ]


def start_halo(pair, bands, sides, corners, sems):
    rows, cols = pair.shape[1:]
    low, high = pl.ds(0, BAND), pl.ds(rows - BAND, BAND)
    left, right = pl.ds(0, LANES), pl.ds(cols - LANES, LANES)
    return [
        send(pair.at[:, low, :], bands.at[0], sems, 0, -1, 0),
        send(pair.at[:, high, :], bands.at[1], sems, 1, 1, 0),
        send(pair.at[:, :, left], sides.at[0], sems, 2, 0, -1),
        send(pair.at[:, :, right], sides.at[1], sems, 3, 0, 1),
        send(pair.at[:, low, left], corners.at[0], sems, 4, -1, -1),
        send(pair.at[:, low, right], corners.at[1], sems, 5, -1, 1),
        send(pair.at[:, high, left], corners.at[2], sems, 6, 1, -1),
        send(pair.at[:, high, right], corners.at[3], sems, 7, 1, 1),
    ]


def lane_index(shape):
    return lax.broadcasted_iota(jnp.int32, shape, len(shape) - 1)


def row_index(shape):
    return lax.broadcasted_iota(jnp.int32, shape, len(shape) - 2)


def joined(which, pair, bands, sides, corners):
    def lanes(own, north, south):
        return jnp.concatenate(
            [own, jnp.where(lane_index(north.shape) < HALF, north, south)], axis=1
        )

    return jnp.concatenate(
        [
            lanes(pair[which], sides[0, which], sides[1, which]),
            lanes(bands[0, which], corners[0, which], corners[1, which]),
            lanes(bands[1, which], corners[2, which], corners[3, which]),
        ],
        axis=0,
    )


def after(field, axis):
    return pltpu.roll(field, field.shape[axis] - 1, axis)


def before(field, axis):
    return pltpu.roll(field, 1, axis)


def around_total(field):
    pair = after(field, 0) + before(field, 0)
    slanted = field + 0.5 * pair
    return pair + after(slanted, 1) + before(slanted, 1)


def inverse_of(value):
    near = pl.reciprocal(value, approx=True)
    return near * (2.0 - value * near)


def fill(k, packed, lane, side, shift):
    return jnp.where(lane == k, pltpu.roll(side, shift, 1), packed)


def by_level(levels, body, carry):
    def step(at, carry):
        for inner in range(GROUP):
            carry = body(at * GROUP + inner, carry)
        return carry

    return lax.fori_loop(0, levels // GROUP, step, carry)


def columns_kernel(
    temp_hbm,
    speed_hbm,
    mix_hbm,
    sea_hbm,
    tally_hbm,
    rain_hbm,
    temp_out,
    speed_out,
    root_out,
    inverse_out,
    source_out,
    totals_out,
    temp,
    east,
    north,
    mix,
    value,
    factor,
    scale,
    sea,
    tally,
    depth,
    depth_e,
    depth_n,
    surf,
    totals,
    tail_ref,
    row_east,
    row_west,
    from_west,
    from_east,
    col_north,
    col_south,
    from_south,
    from_north,
    press_row,
    press_from_east,
    press_col,
    press_from_north,
    last_row_low,
    last_row_rest,
    last_col,
    fix_row,
    fix_col,
    load_sems,
    chunk_sems,
    edge_sems,
    bands,
    sides,
    corners,
    halo_sems,
    total_bands,
    total_sides,
    total_corners,
    total_sems,
):
    levels, rows, cols = temp.shape
    strips = rows // BAND
    greet_neighbours()
    low, high = slice(0, LANES), slice(cols - LANES, cols)
    last_rows, last_lanes = pl.ds(rows - BAND, BAND), pl.ds(cols - LANES, LANES)
    other_rows, other_lanes = pl.ds(0, rows - BAND), pl.ds(0, cols - LANES)
    first_loads = [
        pltpu.make_async_copy(src, dst, load_sems.at[at])
        for at, (src, dst) in enumerate(
            (
                (sea_hbm, sea),
                (tally_hbm, tally),
                (rain_hbm, surf.at[1]),
                (speed_hbm.at[1, :, :, last_lanes], north.at[:, :, last_lanes]),
                (speed_hbm.at[0, :, last_rows, :], east.at[:, last_rows, :]),
            )
        )
    ]
    chunks = levels // GROUP

    def load_temp(at):
        span = pl.ds(at * GROUP, GROUP)
        return pltpu.make_async_copy(temp_hbm.at[span], temp.at[span], chunk_sems.at[3, at])

    for copy in first_loads[:3] + [load_temp(at) for at in range(chunks)] + first_loads[3:]:
        copy.start()

    def load_mix(at):
        span = pl.ds(at * GROUP, GROUP)
        return pltpu.make_async_copy(mix_hbm.at[span], mix.at[span], chunk_sems.at[0, at])

    def load_speeds(at):
        span = pl.ds(at * GROUP, GROUP)
        return [
            pltpu.make_async_copy(
                speed_hbm.at[0, span, other_rows, :],
                east.at[span, other_rows, :],
                chunk_sems.at[1, at],
            ),
            pltpu.make_async_copy(
                speed_hbm.at[1, span, :, other_lanes],
                north.at[span, :, other_lanes],
                chunk_sems.at[2, at],
            ),
        ]

    for at in range(chunks):
        for copy in (load_mix(at), *load_speeds(at)):
            copy.start()
    for copy in first_loads[:3]:
        copy.wait()

    tile = (rows, cols)
    latitude = lax.axis_index("gy") * cols + lane_index(tile)
    inner = (latitude > 0) & (latitude < cols * lax.axis_size("gy") - 1)
    wet_levels = jnp.where(inner & (sea[...] == 1), tally[...], 0).astype(F32)
    depth[...] = wet_levels
    surf[0] = wet_levels
    depth_e[...] = jnp.where(
        row_index(tile) == rows - 1, 0.0, jnp.minimum(wet_levels, after(wet_levels, 0))
    )
    depth_n[...] = jnp.where(
        lane_index(tile) == cols - 1, 0.0, jnp.minimum(wet_levels, after(wet_levels, 1))
    )

    lane = lane_index((rows, LANES))
    zero_side = jnp.zeros((rows, LANES), F32)
    def pack_temp(k, carry):
        to_north, to_south = carry
        one = pl.ds(k, 1)
        row_east[0, one, :] = temp[k, rows - 1 : rows, :]
        row_west[one, :] = temp[k, 0:1, :]
        to_north = fill(k, to_north, lane, temp[k, :, high], k + 1)
        to_south = fill(k, to_south, lane, temp[k, :, low], k)
        return to_north, to_south

    def pack_speed(k, to_north):
        row_east[1, pl.ds(k, 1), :] = east[k, rows - 1 : rows, :]
        return fill(k + HALF, to_north, lane, north[k, :, high], k + 1 + HALF)

    def pack_chunk(at, carry):
        load_temp(at).wait()
        for inner in range(GROUP):
            carry = pack_temp(at * GROUP + inner, carry)
        return carry

    to_north, to_south = lax.fori_loop(0, chunks, pack_chunk, (zero_side, zero_side))
    col_south[...] = to_south
    meet_neighbours()
    surf_copies = start_halo(surf, bands, sides, corners, halo_sems)
    edges = [
        send(row_west, from_east, edge_sems, 0, -1, 0),
        send(col_south, from_north, edge_sems, 1, 0, -1),
    ]
    first_loads[3].wait()
    first_loads[4].wait()
    col_north[...] = by_level(levels, pack_speed, to_north)
    edges += [
        send(row_east, from_west, edge_sems, 2, 1, 0),
        send(col_north, from_south, edge_sems, 3, 0, 1),
    ]

    band = (BAND, cols)
    band_row = row_index(band)

    def upwind(open_depth, level, speed, here, there):
        flux = speed * jnp.where(speed > 0.0, here, there)
        return jnp.where(level < open_depth, flux, 0.0)

    part = [pl.ds(at * BAND, BAND) for at in range(strips)]

    def neighbour_rows(read, at, here, turned):
        if at + 1 == strips:
            return turned, None, None
        later = read(at + 1)
        later_turned = pltpu.roll(later, BAND - 1, 0)
        return jnp.where(band_row == BAND - 1, later_turned, turned), later, later_turned

    def assemble(first, carry):
        ks = [first + at for at in range(QUAD)]
        reads = [lambda at, k=k: temp[k, part[at], :] for k in ks]
        heres = [read(0) for read in reads]
        turns = [pltpu.roll(here, BAND - 1, 0) for here in heres]
        previous = [jnp.zeros(band, F32)] * QUAD
        result = []
        for at in range(strips):
            keep = carry[at]
            wet = depth[part[at], :]
            wet_e = depth_e[part[at], :]
            wet_n = depth_n[part[at], :]
            above = jnp.where(jnp.asarray(first, F32) < wet, mix[first, part[at], :], 0.0)
            for q, k in enumerate(ks):
                level = jnp.asarray(k, F32)
                here = heres[q]
                there, heres[q], next_turn = neighbour_rows(reads[q], at, here, turns[q])
                turns[q] = next_turn
                flux = upwind(wet_e, level, east[k, part[at], :], here, there)
                turned_flux = pltpu.roll(flux, 1, 0)
                total = flux - jnp.where(band_row == 0, previous[q], turned_flux)
                previous[q] = turned_flux
                flux = upwind(wet_n, level, north[k, part[at], :], here, after(here, 1))
                total = total + (flux - before(flux, 1))
                value[k, part[at], :] = here - advect_scale * total
                below = jnp.where(
                    level + 1.0 < wet, mix[jnp.minimum(k + 1, levels - 1), part[at], :], 0.0
                )
                inverse_pivot = inverse_of((1.0 + below) + above * keep)
                scale[k, part[at], :] = inverse_pivot
                leading = below * inverse_pivot
                factor[k, part[at], :] = leading
                keep = 1.0 - leading
                above = below
            result.append(keep)
        return tuple(result)

    def assemble_chunk(at, carry):
        @pl.when(at + 1 < chunks)
        def _():
            load_mix(at + 1).wait()

        for copy in load_speeds(at):
            copy.wait()

        def step(half, carry):
            return assemble(at * GROUP + QUAD * half, carry)

        return lax.fori_loop(0, GROUP // QUAD, step, carry)

    load_mix(0).wait()
    lax.fori_loop(0, chunks, assemble_chunk, (jnp.zeros(band, F32),) * strips)

    for copy in surf_copies:
        copy.wait()
    wide = joined(0, surf, bands, sides, corners)
    last_e = jnp.minimum(wide[rows - 1 : rows, :cols], wide[rows : rows + 1, :cols])
    last_n = jnp.minimum(wide[:rows, cols - 1 : cols], wide[:rows, cols : cols + 1])
    open_w = jnp.minimum(wide[0:1, :cols], wide[-1:, :cols])
    open_s = jnp.minimum(wide[:rows, 0:1], wide[:rows, -1:])

    for copy in edges:
        copy.wait()
    level_row = row_index((levels, cols)).astype(F32)
    level_lane = lane.astype(F32)
    flux_w = upwind(open_w, level_row, from_west[1], from_west[0], row_west[...])
    flux_e = upwind(last_e, level_row, row_east[1], row_east[0], from_east[...])
    flux_s = upwind(
        open_s, level_lane, pltpu.roll(from_south[...], HALF, 1), from_south[...], col_south[...]
    )
    flux_n = upwind(
        last_n, level_lane, pltpu.roll(col_north[...], HALF, 1), col_north[...], from_north[...]
    )
    from_west[0] = advect_scale * flux_w
    from_west[1] = advect_scale * flux_e
    from_south[...] = advect_scale * flux_s
    from_north[...] = advect_scale * flux_n

    rest = cols - LANES
    whole_low = (rows, 0, LANES)
    band_rest = (BAND, LANES, cols)
    whole_rest = (rows, LANES, cols)

    def forward(k, x, region):
        size, start, stop = region
        one = pl.ds(k, 1)
        source = value[k, :size, start:stop]
        if start == 0:
            rim = jnp.where(lane == 0, pltpu.roll(from_south[...], LANES - k, 1), 0.0)
        else:
            turned = pltpu.roll(from_north[:size, :], LANES - 1 - k, 1)
            rim = jnp.where(lane[:size] == LANES - 1, -turned, 0.0)
            if rest > LANES:
                rim = jnp.concatenate([jnp.zeros((size, rest - LANES), F32), rim], axis=1)
        source = source + rim
        row = band_row[:, : stop - start]
        pieces = [source[:BAND] + jnp.where(row == 0, from_west[0, one, :][:, start:stop], 0.0)]
        if size == rows:
            pieces += [
                source[BAND : rows - BAND],
                source[rows - BAND :]
                - jnp.where(row == BAND - 1, from_west[1, one, :][:, start:stop], 0.0),
            ]
        source = jnp.concatenate(pieces, axis=0) if len(pieces) > 1 else pieces[0]
        above = jnp.where(
            jnp.asarray(k, F32) < depth[:size, start:stop], mix[k, :size, start:stop], 0.0
        )
        x = (source + above * x) * scale[k, :size, start:stop]
        temp[k, :size, start:stop] = x
        return x

    slope = force_scale / levels

    def backward(k, x, tail, region):
        size, start, stop = region
        x = temp[k, :size, start:stop] + factor[k, :size, start:stop] * x
        share = slope * x
        tail = tail + share
        press = tail - 0.5 * share
        if size == rows:
            temp_out[k, :, start:stop] = x
            value[k, :, start:stop] = press
            last = last_row_low if start == 0 else last_row_rest
            last[pl.ds(k, 1), :] = press[rows - 1 :, :]
        return x, tail, press

    zero_low = jnp.zeros((rows, LANES), F32)
    zero_band = jnp.zeros((BAND, rest), F32)
    zero_rest = jnp.zeros((rows, rest), F32)

    def forward_first(k, carry):
        return forward(k, carry[0], whole_low), forward(k, carry[1], band_rest)

    def backward_first(step, carry):
        x, tail, x_band, tail_band, packed = carry
        k = levels - 1 - step
        one = pl.ds(k, 1)
        x, tail, press = backward(k, x, tail, whole_low)
        packed = fill(k, packed, lane, press, k)
        x_band, tail_band, press_band = backward(k, x_band, tail_band, band_rest)
        press_row[one, :] = jnp.concatenate([press[0:1, :], press_band[0:1, :]], axis=1)
        return x, tail, x_band, tail_band, packed

    def backward_rest(step, carry):
        x, tail, packed = carry
        k = levels - 1 - step
        x, tail, press = backward(k, x, tail, whole_rest)
        packed = fill(k, packed, lane, press[:, rest - LANES :], k + 1)
        return x, tail, packed

    by_level(levels, forward_first, (zero_low, zero_band))
    x, tail, x_band, tail_band, packed = by_level(
        levels, backward_first, (zero_low, zero_low, zero_band, zero_band, zero_side)
    )
    tail_ref[:, :LANES] = tail
    press_row[:, :LANES] -= tail[0:1, :]
    press_row[:, LANES:] -= tail_band[0:1, :]
    last_row_low[...] -= tail[rows - 1 :, :]
    press_col[...] = packed - tail[:, 0:1]
    press = [
        send(press_row, press_from_east, edge_sems, 4, -1, 0),
        send(press_col, press_from_north, edge_sems, 5, 0, -1),
    ]
    by_level(levels, lambda k, x: forward(k, x, whole_rest), zero_rest)
    x, tail, packed = by_level(levels, backward_rest, (zero_rest, zero_rest, zero_side))
    tail_ref[:, LANES:] = tail
    last_row_rest[...] -= tail[rows - 1 :, :]
    last_col[...] = packed - tail[:, rest - 1 :]

    totals[...] = jnp.zeros(totals.shape, F32)

    def momentum(step, carry):
        ks = [step * QUAD + at for at in range(QUAD)]
        reads = [lambda at, k=k: value[k, part[at], :] - tail_ref[part[at], :] for k in ks]
        heres = [read(0) for read in reads]
        turns = [pltpu.roll(here, BAND - 1, 0) for here in heres]
        for at in range(strips):
            wet_e = depth_e[part[at], :]
            wet_n = depth_n[part[at], :]
            sums = [totals[0, part[at], :], totals[1, part[at], :]]
            for q, k in enumerate(ks):
                level = jnp.asarray(k, F32)
                here = heres[q]
                there, heres[q], next_turn = neighbour_rows(reads[q], at, here, turns[q])
                turns[q] = next_turn
                speed = east[k, part[at], :] + (here - there)
                speed = jnp.where(level < wet_e, speed, 0.0)
                speed_out[0, k, part[at], :] = speed
                sums[0] = sums[0] + speed
                speed = north[k, part[at], :] + (here - after(here, 1))
                speed = jnp.where(level < wet_n, speed, 0.0)
                speed_out[1, k, part[at], :] = speed
                sums[1] = sums[1] + speed
            totals[0, part[at], :] = sums[0]
            totals[1, part[at], :] = sums[1]
        return carry

    lax.fori_loop(0, levels // QUAD, momentum, 0)

    for copy in press:
        copy.wait()
    last_row = jnp.concatenate([last_row_low[...], last_row_rest[...]], axis=1)
    speed_e = row_east[1] + (last_row - press_from_east[...])
    speed_e = jnp.where(level_row < last_e, speed_e, 0.0)
    speed_n = pltpu.roll(col_north[...], HALF, 1) + (last_col[...] - press_from_north[...])
    speed_n = jnp.where(level_lane < last_n, speed_n, 0.0)
    fix_row[...] = speed_e
    fix_col[...] = speed_n
    totals[0, rows - 1 : rows, :] = jnp.sum(speed_e, axis=0, keepdims=True)
    totals[1, :, high] += jnp.where(
        lane == LANES - 1, jnp.sum(speed_n, axis=1, keepdims=True), 0.0
    )
    total_copies = start_halo(totals, total_bands, total_sides, total_corners, total_sems)

    def add_last(k, carry):
        speed_out[0, k, rows - 1 : rows, :] = fix_row[pl.ds(k, 1), :]
        speed_out[1, k, :, high] += jnp.where(
            lane == LANES - 1, pltpu.roll(fix_col[...], LANES - 1 - k, 1), 0.0
        )
        return carry

    by_level(levels, add_last, 0)

    root = jnp.sqrt(wide / levels)
    inverse = 1.0 / (damping + root * around_total(root))
    root_out[...] = root
    inverse_out[...] = inverse
    source_out[...] = source_scale * joined(1, surf, bands, sides, corners)

    for copy in total_copies:
        copy.wait()
    for which in range(2):
        totals_out[which] = joined(which, totals, total_bands, total_sides, total_corners)


def surface_kernel(
    temp_in,
    speed_in,
    root_in,
    inverse_in,
    source_in,
    totals_in,
    temp_out,
    speed_out,
    out,
    sems,
):
    rows, cols = out.shape
    levels = temp_in.shape[0]
    copies = [
        pltpu.make_async_copy(temp_in, temp_out, sems.at[0]),
        pltpu.make_async_copy(speed_in.at[0], speed_out.at[0], sems.at[1]),
        pltpu.make_async_copy(speed_in.at[1], speed_out.at[1], sems.at[2]),
    ]
    for copy in copies:
        copy.start()
    root = root_in[...]
    inverse = inverse_in[...]
    ratio = root * inverse
    total_e, total_n = totals_in[0], totals_in[1]
    divergence = total_e - before(total_e, 0) + total_n - before(total_n, 1)
    forcing = source_in[...] - (divergence_scale / levels) * divergence
    scaled = jnp.where(root > 0.0, forcing * inverse, 0.0)
    update = scaled * (1.0 / cheb_gamma)
    iterate = update
    omega = 2.0 / cheb_gamma
    for _ in range(1, ITERS):
        omega = 1.0 / (cheb_gamma - omega / (4.0 * cheb_alpha * cheb_alpha))
        residual = scaled - iterate + ratio * around_total(root * iterate)
        update = omega * residual + (cheb_gamma * omega - 1.0) * update
        iterate = iterate + update
    out[...] = iterate[:rows, :cols]
    for copy in copies:
        copy.wait()


def local(temp, speeds, mix, sea, tally, rain):
    levels, rows, cols = temp.shape
    wide = pltpu.VMEM((rows + 2 * BAND, cols + LANES), F32)
    wide_pair = pltpu.VMEM((2, rows + 2 * BAND, cols + LANES), F32)
    vmem = pl.BlockSpec(memory_space=pltpu.VMEM)
    field = pltpu.VMEM((levels, rows, cols), F32)
    plane = pltpu.VMEM((rows, cols), F32)
    plane_int = pltpu.VMEM((rows, cols), jnp.int32)
    two_planes = pltpu.VMEM((2, rows, cols), F32)
    row_set = pltpu.VMEM((levels, cols), F32)
    row_sets = pltpu.VMEM((2, levels, cols), F32)
    col_set = pltpu.VMEM((rows, LANES), F32)
    inputs = [
        pltpu.with_memory_space_constraint(array, pltpu.HBM)
        for array in (temp, speeds, mix, sea, tally, rain)
    ]
    results = pl.pallas_call(
        columns_kernel,
        out_shape=[field, pltpu.VMEM((2, levels, rows, cols), F32), wide, wide, wide, wide_pair],
        in_specs=[pl.BlockSpec(memory_space=pltpu.HBM)] * 6,
        out_specs=[vmem] * 6,
        scratch_shapes=[field] * 7
        + [plane_int] * 2
        + [plane] * 3
        + [two_planes, two_planes, plane]
        + [row_sets, row_set, row_sets, row_set]
        + [col_set] * 4
        + [row_set, row_set, col_set, col_set]
        + [pltpu.VMEM((levels, LANES), F32), pltpu.VMEM((levels, cols - LANES), F32), col_set]
        + [row_set, col_set]
        + [
            pltpu.SemaphoreType.DMA((5,)),
            pltpu.SemaphoreType.DMA((4, levels // GROUP)),
            pltpu.SemaphoreType.DMA((2, 6)),
        ]
        + halo_shapes(rows, cols) * 2,
        compiler_params=pltpu.CompilerParams(
            collective_id=0, has_side_effects=True, vmem_limit_bytes=48 * 2**20
        ),
        name="columns",
    )(*inputs)
    held = [
        pltpu.with_memory_space_constraint(array, pltpu.VMEM)
        for array in results
    ]
    return pl.pallas_call(
        surface_kernel,
        out_shape=[
            jax.ShapeDtypeStruct(temp.shape, F32),
            jax.ShapeDtypeStruct(speeds.shape, F32),
            jax.ShapeDtypeStruct((rows, cols), F32),
        ],
        in_specs=[vmem] * 6,
        out_specs=[pl.BlockSpec(memory_space=pltpu.HBM)] * 2 + [vmem],
        scratch_shapes=[pltpu.SemaphoreType.DMA((3,))],
        compiler_params=pltpu.CompilerParams(vmem_limit_bytes=32 * 2**20),
        name="surface",
    )(*held)


def solution(mesh):
    tile = P("gx", "gy")
    column = P(None, "gx", "gy")
    pair = P(None, None, "gx", "gy")
    return jax.shard_map(
        local,
        mesh=mesh,
        in_specs=(column, pair, column, tile, tile, tile),
        out_specs=(column, pair, tile),
        check_vma=False,
    )
```
